32 devices in a mesh: dp: 8 (over z, x), tensor: 4 (over y, core).
Axes of the slice: x: 2, y: 2, z: 4, core: 2. Of those that a mesh axis runs over, the one named last changes fastest.
Arguments:
- tokens: bfloat16 [16384, 1024], P(('dp', 'tensor')), may hold values from -6 to 6
- norm_gain: bfloat16 [1024], P('dp'), may hold values from 0.5 to 1.5
- query_weight: bfloat16 [1024, 512], P('dp', 'tensor'), may hold values from -0.1875 to 0.1875
- key_weight: bfloat16 [1024, 512], P('dp', 'tensor'), may hold values from -0.1875 to 0.1875
- value_weight: bfloat16 [1024, 1024], P('dp', 'tensor'), may hold values from -0.1875 to 0.1875
- gate_weight: bfloat16 [1024, 1024], P('dp', 'tensor'), may hold values from -0.1875 to 0.1875
- low_down: bfloat16 [1024, 16], P('dp'), may hold values from -0.1875 to 0.1875
- low_up: bfloat16 [4, 16, 128], P('tensor', None, 'dp'), may hold values from -1.5 to 1.5
- rank_bias: bfloat16 [4, 128], P('tensor', 'dp'), may hold values from -1 to 7
- head_gain: bfloat16 [256], P('dp'), may hold values from 0.5 to 1.5
- out_weight: bfloat16 [1024, 1024], P('tensor', 'dp'), may hold values from -0.375 to 0.375
- mlp_gain: bfloat16 [1024], P('dp'), may hold values from 0.5 to 1.5
- mlp_gate: bfloat16 [1024, 2816], P('dp', 'tensor'), may hold values from -0.1875 to 0.1875
- mlp_up: bfloat16 [1024, 2816], P('dp', 'tensor'), may hold values from -0.1875 to 0.1875
- mlp_down: bfloat16 [2816, 1024], P('tensor', 'dp'), may hold values from -0.15625 to 0.15625
- cotangent: bfloat16 [16384, 1024], P(('dp', 'tensor')), may hold values from -6 to 6
Outputs:
- block_out: bfloat16 [16384, 1024], P(('dp', 'tensor'))
- grad_tokens: float32 [16384, 1024], P(('dp', 'tensor'))
- grad_norm_gain: float32 [1024], P(('dp', 'tensor'))
- grad_query: float32 [1024, 512], P('dp', 'tensor')
- grad_key: float32 [1024, 512], P('dp', 'tensor')
- grad_value: float32 [1024, 1024], P('dp', 'tensor')
- grad_gate: float32 [1024, 1024], P('dp', 'tensor')
- grad_low_down: float32 [1024, 16], P(('dp', 'tensor'))
- grad_low_up: float32 [4, 16, 128], P('tensor', None, 'dp')
- grad_rank_bias: float32 [4, 128], P('tensor', 'dp')
- grad_head_gain: float32 [256], P(('dp', 'tensor'))
- grad_out_weight: float32 [1024, 1024], P('tensor', 'dp')
- grad_mlp_gain: float32 [1024], P(('dp', 'tensor'))
- grad_mlp_gate: float32 [1024, 2816], P('dp', 'tensor')
- grad_mlp_up: float32 [1024, 2816], P('dp', 'tensor')
- grad_mlp_down: float32 [2816, 1024], P('tensor', 'dp')
The draws below stay inside these ranges and needn't reach their ends.
All inputs are finite; a program needn't handle non-finite values.
Results may differ from the reference program's by a relative error of at most 0.024.
Values may be sent and summed in bfloat16 or wider, within the bound.
No kernel may reach another device: no remote copies, remote signals or barrier semaphores. Data moves between devices by JAX's collectives and lax.ppermute only.
A program may use at most 192 MiB of HBM per device.

```python
import jax
import jax.numpy as jnp
from jax import lax

D = 1024
HEADS = 4
HEAD_K = 128
HEAD_V = 256
FF = 2816
RANK = 16
BLOCK = 64
LEN = 2048
TOKENS = 16384
N_DP = 8


def level_of(stream_key, shape, split, low, largest):
    level = 1.0
    for position, parts in split:
        draws = jax.random.uniform(jax.random.fold_in(jax.random.fold_in(stream_key, 6), position), (parts,), jnp.float32, low / len(split), largest / len(split))
        level = level * jnp.repeat(jnp.exp(draws), shape[position] // parts).reshape((-1,) + (1,) * (len(shape) - 1 - position))
    return level


def gaussian(key, dims, deviation, reach, shards=(), kind=jnp.bfloat16):
    loudness = level_of(key, dims, shards, -0.22, 0.18) if shards else 1.0
    drawn = jax.random.normal(key, dims, jnp.float32) * deviation * loudness
    return jnp.minimum(jnp.maximum(drawn, -reach), reach).astype(kind)


def setup_inputs(seed: int = 0) -> dict:
    key_of = jax.random.split(jax.random.key(seed), 17)
    tokens = gaussian(key_of[0], (TOKENS, D), 1.0, 6.0, ((0, 32),))
    norm_gain = jnp.clip(1.0 + 0.1 * jax.random.normal(key_of[1], (D,), jnp.float32), 0.5, 1.5).astype(jnp.bfloat16)
    query_weight = gaussian(key_of[2], (D, HEADS * HEAD_K), D ** -0.5, 0.1875, ((0, 8), (1, 4)))
    key_weight = gaussian(key_of[3], (D, HEADS * HEAD_K), D ** -0.5, 0.1875, ((0, 8), (1, 4)))
    value_weight = gaussian(key_of[4], (D, HEADS * HEAD_V), D ** -0.5, 0.1875, ((0, 8), (1, 4)))
    gate_weight = gaussian(key_of[5], (D, HEADS * HEAD_V), D ** -0.5, 0.1875, ((0, 8), (1, 4)))
    low_down = gaussian(key_of[6], (D, RANK), D ** -0.5, 0.1875, ((0, 8),))
    low_up = gaussian(key_of[7], (HEADS, RANK, HEAD_K), RANK ** -0.5, 1.5, ((0, 4), (2, 8)))
    rank_bias = jnp.clip(-1.0 + 8.0 * jax.random.uniform(key_of[8], (HEADS, HEAD_K), jnp.float32) ** level_of(key_of[8], (HEADS, HEAD_K), ((0, 4), (1, 8)), -0.2, 0.2), -1.0, 7.0).astype(jnp.bfloat16)
    head_gain = jnp.clip(1.0 + 0.1 * jax.random.normal(key_of[9], (HEAD_V,), jnp.float32), 0.5, 1.5).astype(jnp.bfloat16)
    out_weight = gaussian(key_of[10], (HEADS * HEAD_V, D), HEAD_V ** -0.5, 0.375, ((0, 4), (1, 8)))
    mlp_gain = jnp.clip(1.0 + 0.1 * jax.random.normal(key_of[11], (D,), jnp.float32), 0.5, 1.5).astype(jnp.bfloat16)
    mlp_gate = gaussian(key_of[12], (D, FF), D ** -0.5, 0.1875, ((0, 8), (1, 4)))
    mlp_up = gaussian(key_of[13], (D, FF), D ** -0.5, 0.1875, ((0, 8), (1, 4)))
    mlp_down = gaussian(key_of[14], (FF, D), (FF // 2) ** -0.5, 0.15625, ((0, 4), (1, 8)))
    cotangent = gaussian(key_of[15], (TOKENS, D), 1.0, 6.0, ((0, 32),))
    return {"tokens": tokens, "norm_gain": norm_gain, "query_weight": query_weight, "key_weight": key_weight, "value_weight": value_weight, "gate_weight": gate_weight, "low_down": low_down, "low_up": low_up, "rank_bias": rank_bias, "head_gain": head_gain, "out_weight": out_weight, "mlp_gain": mlp_gain, "mlp_gate": mlp_gate, "mlp_up": mlp_up, "mlp_down": mlp_down, "cotangent": cotangent}


@jax.custom_vjp
def low(v):
    return lax.optimization_barrier(v.astype(jnp.bfloat16)).astype(jnp.float32)

@jax.custom_vjp
def low_back(v):
    return v

def low_keep(v):
    return (low(v), None)

def low_pass(kept, grad):
    return (grad,)

def back_keep(v):
    return (v, None)

def back_low(kept, grad):
    return (low(grad),)
low.defvjp(low_keep, low_pass)
low_back.defvjp(back_keep, back_low)
TOP_PRECISION = lax.Precision.HIGHEST
NORM_EPS = 1e-06
HEAD_EPS = 1e-05
NORMALIZER = 16.0

def product(former, latter):
    return jnp.dot(former, latter, precision=TOP_PRECISION)

def rms_scale(values, epsilon):
    return lax.rsqrt(lax.optimization_barrier(jnp.mean(values * values, axis=-1, keepdims=True)) + epsilon)

def token_step(running_memory, token_data):
    query_slice_row, key_row, value_row, decay_row = token_data
    running_memory = jnp.exp(decay_row)[:, :, None] * running_memory + key_row[:, :, None] * value_row[:, None, :]
    return (running_memory, jnp.einsum('sn,snj->sj', query_slice_row, running_memory, precision=TOP_PRECISION))

def block_step(running_memory, block_data):
    return lax.scan(token_step, running_memory, block_data)

def recurrence(queries, key_rows, values, decays):
    length = queries.shape[0]

    def blocked(source):
        return source.reshape((length // BLOCK, BLOCK) + source.shape[1:])
    initial = jnp.zeros((HEADS, HEAD_K, HEAD_V), jnp.float32)
    _, final_result = lax.scan(jax.checkpoint(block_step), initial, (blocked(queries), blocked(key_rows), blocked(values), blocked(decays)))
    return final_result.reshape(length, HEADS, HEAD_V)

def block_layer(inputs, norm_gain, query_weight, key_weight, value_weight, gate_weight, low_down, low_up, rank_bias, head_gain, out_weight, mlp_gain, mlp_gate, mlp_up, mlp_down):
    length = inputs.shape[0]
    normed = low(inputs * rms_scale(inputs, NORM_EPS) * norm_gain)
    queries = low(low_back(product(normed, query_weight)))
    key_rows = low(low_back(product(normed, key_weight)))
    values = low(low_back(product(normed, value_weight)))
    gate_in = low_back(product(normed, gate_weight))
    low_rank = low_back(product(normed, low_down))
    logits = jnp.einsum('lr,hrk->lhk', low_rank, low_up, precision=TOP_PRECISION) + rank_bias
    decays = jax.nn.log_sigmoid(logits) / NORMALIZER
    mixed_heads = recurrence(queries.reshape(length, HEADS, HEAD_K), key_rows.reshape(length, HEADS, HEAD_K), values.reshape(length, HEADS, HEAD_V), decays) * HEAD_K ** (-0.5)
    gated_heads = mixed_heads * rms_scale(mixed_heads, HEAD_EPS) * head_gain * jax.nn.silu(gate_in.reshape(length, HEADS, HEAD_V))
    mixer_out = low_back(product(low(gated_heads.reshape(length, HEADS * HEAD_V)), out_weight))
    middle = inputs + mixer_out
    second = low(middle * rms_scale(middle, NORM_EPS) * mlp_gain)
    gate_pre = low_back(product(second, mlp_gate))
    up_pre = low_back(product(second, mlp_up))
    hidden = low(jax.nn.silu(gate_pre) * up_pre)
    return middle + low_back(product(hidden, mlp_down))

def reference(tokens, norm_gain, query_weight, key_weight, value_weight, gate_weight, low_down, low_up, rank_bias, head_gain, out_weight, mlp_gain, mlp_gate, mlp_up, mlp_down, cotangent):
    weights = tuple((weight_arg.astype(jnp.float32) for weight_arg in (norm_gain, query_weight, key_weight, value_weight, gate_weight, low_down, low_up, rank_bias, head_gain, out_weight, mlp_gain, mlp_gate, mlp_up, mlp_down)))
    inputs = tokens.astype(jnp.float32).reshape(N_DP, LEN, D)
    cotangents = cotangent.astype(jnp.float32).reshape(N_DP, LEN, D)

    def per_sequence(totals, sequence_pair):
        sequence, seq_cot = sequence_pair
        final_result, pullback = jax.vjp(block_layer, sequence, *weights)
        gradients = pullback(seq_cot)
        totals = tuple((running + piece_grad for running, piece_grad in zip(totals, gradients[1:])))
        return (totals, (final_result.astype(jnp.bfloat16), gradients[0]))
    initial = tuple((jnp.zeros_like(weight_arg) for weight_arg in weights))
    totals, (outputs, input_grads) = lax.scan(per_sequence, initial, (inputs, cotangents))
    return (outputs.reshape(TOKENS, D), input_grads.reshape(TOKENS, D), totals[0], totals[1], totals[2], totals[3], totals[4], totals[5], totals[6], totals[7], totals[8], totals[9], totals[10], totals[11], totals[12], totals[13])
```

```python
import jax
import jax.numpy as jnp
from jax import lax
from jax.experimental import pallas as pl
from jax.experimental.pallas import tpu as pltpu
from jax.sharding import PartitionSpec as P

HEAD_K = 128
HEAD_V = 256
CHUNK = 128
FF_ROWS = 256
LANES = 128
SAFE_RANGE = 60.0

TOP_PRECISION = lax.Precision.HIGHEST
NORM_EPS = 1e-06
HEAD_EPS = 1e-05
NORMALIZER = 16.0
CORE = 1
PAIR = 2
BF = jnp.bfloat16
F32 = jnp.float32


def swap(array, axis, mask):
    size = lax.axis_size(axis)
    return lax.ppermute(array, axis, [(i, i ^ mask) for i in range(size)])


def radices(count):
    result = []
    while count > 1:
        radix = 4 if count % 4 == 0 else 2
        result.append(radix)
        count //= radix
    return result


def gather(part):
    span, held = 2, part
    for radix in radices(lax.axis_size("dp") // 2):
        held = jnp.concatenate([held] + [swap(held, "dp", d * span) for d in range(1, radix)], axis=0)
        span *= radix
    half = held.shape[0] // 2
    beside = swap(held, "dp", 1)
    pair = swap(held, "tensor", PAIR)
    pair_low = swap(pair[:half], "dp", 1)
    pair_high = swap(beside[half:], "tensor", PAIR)
    return (held, beside), (pair, pair_low, pair_high)


def scatter(own, pair):
    count = own.shape[0] // 2
    half = count // 2
    pair_low = swap(pair[count : count + half], "dp", 1)
    own_high = swap(pair[count + half :], "tensor", PAIR)
    total = own[:count].astype(F32)
    beside_low = swap(own[count : count + half], "dp", 1)
    pair_rest = swap(pair[half:count], "tensor", PAIR)
    beside_high = swap(
        (own[count + half :].astype(F32) + own_high.astype(F32)).astype(BF), "dp", 1
    )
    pair_sum = swap((pair[:half].astype(F32) + pair_low.astype(F32)).astype(BF), "tensor", PAIR)
    total = total + jnp.concatenate([beside_low, beside_high], axis=0).astype(F32)
    total = total + jnp.concatenate([pair_sum, pair_rest], axis=0).astype(F32)
    spans, span = [], 2
    for radix in radices(lax.axis_size("dp") // 2):
        spans.append((radix, span))
        span *= radix
    for radix, span in reversed(spans):
        rows = total.shape[0] // radix
        low = total.astype(BF)
        arrived = [swap(low[d * rows : (d + 1) * rows], "dp", d * span) for d in range(1, radix)]
        total = total[:rows] + sum(a.astype(F32) for a in arrived)
    return total


def place_matrix(width):
    count = lax.axis_size("dp")
    block = width // count
    feature = lax.broadcasted_iota(jnp.int32, (width, width), 0)
    place = lax.broadcasted_iota(jnp.int32, (width, width), 1)
    slot = place // block
    owner = (slot % (count // 2) * 2 + slot // (count // 2)) ^ lax.axis_index("dp")
    return (feature == owner * block + place % block).astype(BF)


def block_matrix():
    count = lax.axis_size("dp")
    owner = lax.broadcasted_iota(jnp.int32, (count, count), 0)
    slot = lax.broadcasted_iota(jnp.int32, (count, count), 1)
    return (owner == ((slot % (count // 2) * 2 + slot // (count // 2)) ^ lax.axis_index("dp"))).astype(F32)


def contract_rows(former, latter):
    return lax.dot_general(former, latter, (((0,), (0,)), ((), ())), preferred_element_type=F32)


def contract_last(former, latter):
    return lax.dot_general(former, latter, (((1,), (1,)), ((), ())), preferred_element_type=F32)


def project(former, latter):
    return jnp.dot(former, latter, preferred_element_type=F32)


def exact(former, latter):
    return jnp.dot(former, latter, preferred_element_type=F32, precision=TOP_PRECISION)


def positions():
    row = lax.broadcasted_iota(jnp.int32, (CHUNK, CHUNK), 0)
    col = lax.broadcasted_iota(jnp.int32, (CHUNK, CHUNK), 1)
    return row, col


def level_terms(cum, size):
    row, col = positions()
    boundary = row // (2 * size) * (2 * size) + size - 1
    at_boundary = exact((col == boundary).astype(F32), cum)
    fade = jnp.exp(-jnp.abs(cum - at_boundary))
    same = row // (2 * size) == col // (2 * size)
    mask = same & (row % (2 * size) >= size) & (col % (2 * size) < size)
    return fade, mask


def state_kernel(shift, k_own, v_own, k_pair, v_pair, low, up, bias, logits, cums, starts, end, memory):
    n = pl.program_id(0)

    @pl.when(n == 0)
    def _():
        memory[...] = jnp.zeros_like(memory)

    row, col = positions()
    triangle = (row >= col).astype(F32)
    for h, (k_ref, v_ref) in enumerate(((k_own, v_own), (k_pair, v_pair))):
        columns = slice(h * HEAD_K, (h + 1) * HEAD_K)
        logit = exact(low[...], up[h]) + bias[h]
        decay = (jnp.minimum(logit, 0.0) - jnp.log1p(jnp.exp(-jnp.abs(logit)))) / NORMALIZER
        cum = exact(triangle, decay)
        closing = cum[CHUNK - 1 :, :]
        logits[:, columns] = logit
        cums[:, columns] = cum
        starts[0, h] = memory[h]
        faded = (k_ref[...].astype(BF).astype(F32) * jnp.exp(closing - cum)).astype(BF)
        memory[h] = jnp.exp(closing) * memory[h] + contract_rows(v_ref[...].astype(BF), faded)

    @pl.when(n == pl.num_programs(0) - 1)
    def _():
        end[...] = memory[...]


def mix_kernel(
    shift, q_own, k_own, v_own, g_own, q_pair, k_pair, v_pair, g_pair, cums, starts, arrived, gain,
    gated_own, gated_pair, mixed_out, full, scores, passed,
):
    n = pl.program_id(0)

    @pl.when(n == 0)
    def _():
        passed[...] = jnp.zeros_like(passed)

    row, col = positions()
    heads = ((q_own, k_own, v_own, g_own, gated_own), (q_pair, k_pair, v_pair, g_pair, gated_pair))
    lowest = jnp.min(cums[CHUNK - 1 :, :])

    @pl.when(lowest > -SAFE_RANGE)
    def _():
        for h, (q_ref, k_ref, _, _, _) in enumerate(heads):
            cum = cums[:, h * HEAD_K : (h + 1) * HEAD_K]
            middle = cum[CHUNK // 2 : CHUNK // 2 + 1, :]
            q = q_ref[...].astype(BF).astype(F32)
            k = k_ref[...].astype(BF).astype(F32)
            both = contract_last((q * jnp.exp(cum - middle)).astype(BF), (k * jnp.exp(middle - cum)).astype(BF))
            scores[h] = jnp.where(row >= col, both, 0.0)

    @pl.when(lowest <= -SAFE_RANGE)
    def _():
        for h, (q_ref, k_ref, _, _, _) in enumerate(heads):
            cum = cums[:, h * HEAD_K : (h + 1) * HEAD_K]
            q = q_ref[...].astype(BF).astype(F32)
            k = k_ref[...].astype(BF).astype(F32)
            scores[h] = jnp.where(row == col, jnp.sum(q * k, axis=1, keepdims=True), 0.0)

            def level(step, carry):
                fade, mask = level_terms(cum, jnp.int32(1) << step)
                both = contract_last((q * fade).astype(BF), (k * fade).astype(BF))
                scores[h] = scores[h] + jnp.where(mask, both, 0.0)
                return carry

            lax.fori_loop(0, CHUNK.bit_length() - 1, level, 0)

    for h, (q_ref, _, v_ref, g_ref, out) in enumerate(heads):
        cum = cums[:, h * HEAD_K : (h + 1) * HEAD_K]
        state = (starts[0, h] + jnp.exp(passed[h]) * arrived[h]).astype(BF)
        full[0, h] = state
        passed[h] = passed[h] + cum[CHUNK - 1 :, :]
        q = q_ref[...].astype(BF).astype(F32)
        mixed = project(scores[h].astype(BF), v_ref[...].astype(BF))
        mixed = mixed + contract_last((q * jnp.exp(cum)).astype(BF), state)
        mixed = mixed * HEAD_K**-0.5
        mixed_out[:, h * HEAD_V : (h + 1) * HEAD_V] = mixed
        scale = lax.rsqrt(jnp.mean(mixed * mixed, axis=-1, keepdims=True) + HEAD_EPS)
        g = g_ref[...]
        out[...] = (mixed * scale * gain[...] * g * jax.nn.sigmoid(g)).astype(BF)


def gate_back_kernel(
    shift, q_own, g_own, d_own, q_pair, g_pair, d_pair, cums, mixed_in, gain,
    d_mixed, d_gate, ends, first, d_gain, memory,
):
    n = pl.program_id(0)

    @pl.when(n == 0)
    def _():
        memory[...] = jnp.zeros_like(memory)
        d_gain[...] = jnp.zeros_like(d_gain)

    for h, (q_ref, g_ref, d_ref) in enumerate(((q_own, g_own, d_own), (q_pair, g_pair, d_pair))):
        wide = slice(h * HEAD_V, (h + 1) * HEAD_V)
        cum = cums[:, h * HEAD_K : (h + 1) * HEAD_K]
        mixed = mixed_in[:, wide]
        scale = lax.rsqrt(jnp.mean(mixed * mixed, axis=-1, keepdims=True) + HEAD_EPS)
        normal = mixed * scale
        g, grad = g_ref[...], d_ref[...]
        sigmoid = jax.nn.sigmoid(g)
        silu = g * sigmoid
        d_gain[...] += jnp.sum(grad * normal * silu, axis=0, keepdims=True)
        scaled = grad * gain[...]
        d_gate[:, wide] = (scaled * normal * sigmoid * (1.0 + g * (1.0 - sigmoid))).astype(BF)
        scaled = scaled * silu
        back = scale * (scaled - normal * jnp.mean(scaled * normal, axis=-1, keepdims=True))
        back = (back * HEAD_K**-0.5).astype(BF)
        d_mixed[:, wide] = back
        ends[0, h] = memory[h]
        q = q_ref[...].astype(BF).astype(F32)
        faded = (q * jnp.exp(cum)).astype(BF)
        memory[h] = jnp.exp(cum[CHUNK - 1 :, :]) * memory[h] + contract_rows(back, faded)

    @pl.when(n == pl.num_programs(0) - 1)
    def _():
        first[...] = memory[...]


def mix_back_kernel(
    shift, q_own, k_own, v_own, low, q_pair, k_pair, v_pair, cums, logits, full, ends, arrived, up,
    d_mixed, d_gate, back_own, back_pair, d_up, d_bias, d_q, d_k, scores, grads, passed,
):
    n = pl.program_id(0)

    @pl.when(n == 0)
    def _():
        passed[...] = jnp.zeros_like(passed)
        d_up[...] = jnp.zeros_like(d_up)
        d_bias[...] = jnp.zeros_like(d_bias)

    row, col = positions()
    heads = ((q_own, k_own, v_own, back_own), (q_pair, k_pair, v_pair, back_pair))
    lowest = jnp.min(cums[CHUNK - 1 :, :])
    for h, (_, _, v_ref, _) in enumerate(heads):
        back = d_mixed[:, h * HEAD_V : (h + 1) * HEAD_V]
        grads[h] = contract_last(back, v_ref[...].astype(BF))

    @pl.when(lowest > -SAFE_RANGE)
    def _():
        for h, (q_ref, k_ref, _, _) in enumerate(heads):
            cum = cums[:, h * HEAD_K : (h + 1) * HEAD_K]
            middle = cum[CHUNK // 2 : CHUNK // 2 + 1, :]
            q = q_ref[...].astype(BF).astype(F32)
            k = k_ref[...].astype(BF).astype(F32)
            rise, fall = jnp.exp(cum - middle), jnp.exp(middle - cum)
            q_faded, k_faded = (q * rise).astype(BF), (k * fall).astype(BF)
            scores[h] = jnp.where(row >= col, contract_last(q_faded, k_faded), 0.0)
            strict = jnp.where(row > col, grads[h], 0.0).astype(BF)
            d_q[h] = project(strict, k_faded) * rise
            d_k[h] = contract_rows(strict, q_faded) * fall

    @pl.when(lowest <= -SAFE_RANGE)
    def _():
        for h, (q_ref, k_ref, _, _) in enumerate(heads):
            cum = cums[:, h * HEAD_K : (h + 1) * HEAD_K]
            q = q_ref[...].astype(BF).astype(F32)
            k = k_ref[...].astype(BF).astype(F32)
            scores[h] = jnp.where(row == col, jnp.sum(q * k, axis=1, keepdims=True), 0.0)
            d_q[h] = jnp.zeros((CHUNK, HEAD_K), F32)
            d_k[h] = jnp.zeros((CHUNK, HEAD_K), F32)

            def level(step, carry):
                fade, mask = level_terms(cum, jnp.int32(1) << step)
                q_faded, k_faded = (q * fade).astype(BF), (k * fade).astype(BF)
                scores[h] = scores[h] + jnp.where(mask, contract_last(q_faded, k_faded), 0.0)
                crossing = jnp.where(mask, grads[h], 0.0).astype(BF)
                d_q[h] = d_q[h] + project(crossing, k_faded) * fade
                d_k[h] = d_k[h] + contract_rows(crossing, q_faded) * fade
                return carry

            lax.fori_loop(0, CHUNK.bit_length() - 1, level, 0)

    later = (row <= col).astype(F32)
    d_low = jnp.zeros((CHUNK, LANES), F32)
    for h, (q_ref, k_ref, v_ref, out) in enumerate(heads):
        columns = slice(h * HEAD_K, (h + 1) * HEAD_K)
        wide = slice(h * HEAD_V, (h + 1) * HEAD_V)
        cum = cums[:, columns]
        closing = cum[CHUNK - 1 :, :]
        q = q_ref[...].astype(BF).astype(F32)
        k = k_ref[...].astype(BF).astype(F32)
        v, back, state = v_ref[...].astype(BF), d_mixed[:, wide], full[0, h]
        state_grad = ends[0, h] + jnp.exp(passed[h]) * arrived[h]
        passed[h] = passed[h] + closing
        low_grad = state_grad.astype(BF)
        fade = jnp.exp(closing - cum)
        q_strict = d_q[h] + project(back, state) * jnp.exp(cum)
        k_state = project(v, low_grad) * fade
        k_strict = d_k[h] + k_state
        diagonal = jnp.sum(jnp.where(row == col, grads[h], 0.0), axis=1, keepdims=True)
        d_v = contract_rows(scores[h].astype(BF), back) + contract_last((k * fade).astype(BF), low_grad)
        d_closing = jnp.sum(k * k_state, axis=0, keepdims=True) + jnp.exp(closing) * jnp.sum(
            state.astype(F32) * state_grad, axis=0, keepdims=True
        )
        d_decay = exact(later, q * q_strict - k * k_strict) + d_closing
        d_logit = d_decay * (jax.nn.sigmoid(-logits[:, columns]) / NORMALIZER)
        out[:, :HEAD_K] = (q_strict + diagonal * k).astype(BF)
        out[:, HEAD_K : 2 * HEAD_K] = (k_strict + diagonal * q).astype(BF)
        out[:, 2 * HEAD_K : 2 * HEAD_K + HEAD_V] = d_v.astype(BF)
        out[:, 2 * HEAD_K + HEAD_V : 2 * HEAD_K + 2 * HEAD_V] = d_gate[:, wide]
        low_logit = d_logit.astype(BF)
        d_low = d_low + contract_last(low_logit, up[h].astype(BF))
        d_up[h] = d_up[h] + contract_rows(low[...].astype(BF), low_logit)
        d_bias[h] = d_bias[h] + jnp.sum(d_logit, axis=0, keepdims=True)
    back_own[:, 2 * HEAD_K + 2 * HEAD_V :] = d_low.astype(BF)


def whole(shape):
    return pl.BlockSpec(shape, lambda n, shift: (0,) * len(shape))


def call(kernel, steps, ins, outs, scratch, flops, arrays, shift, backward=False):
    def at(n):
        return steps - 1 - n if backward else n

    def spec(entry):
        shape, kind, column = entry
        if kind == "r":
            return pl.BlockSpec(shape, lambda n, shift: ((at(n) + shift[0]) % steps, column))
        if kind == "t":
            return pl.BlockSpec(shape, lambda n, shift: (at(n),) + (0,) * (len(shape) - 1))
        return whole(shape)

    shapes = []
    for (shape, kind, _), dtype in outs:
        shapes.append(jax.ShapeDtypeStruct((shape[0] * (steps if kind != "w" else 1),) + shape[1:], dtype))
    return pl.pallas_call(
        kernel,
        grid_spec=pltpu.PrefetchScalarGridSpec(
            num_scalar_prefetch=1,
            grid=(steps,),
            in_specs=[spec(entry) for entry in ins],
            out_specs=[spec(entry) for entry, _ in outs],
            scratch_shapes=scratch,
        ),
        out_shape=shapes,
        compiler_params=pltpu.CompilerParams(vmem_limit_bytes=40 << 20),
        cost_estimate=pl.CostEstimate(flops=flops, bytes_accessed=12 << 20, transcendentals=0),
    )(shift, *arrays)


NARROW, WIDE = (CHUNK, HEAD_K), (CHUNK, HEAD_V)
STATES = (1, 2, HEAD_V, HEAD_K)
Q, K, V, G = (NARROW, "r", 0), (NARROW, "r", 1), (WIDE, "r", 1), (WIDE, "r", 2)
LOW = (NARROW, "r", (2 * HEAD_K + 2 * HEAD_V) // LANES)
CUMS = ((CHUNK, 2 * HEAD_K), "t", 0)
HEADS_WIDE = ((CHUNK, 2 * HEAD_V), "t", 0)
STATE = ((2, HEAD_V, HEAD_K), "w", 0)
SQUARES = pltpu.VMEM((2, CHUNK, CHUNK), F32)
MEMORY = pltpu.VMEM((2, HEAD_V, HEAD_K), F32)
PASSED = pltpu.VMEM((2, 1, HEAD_K), F32)
UP = ((2, LANES, HEAD_K), "w", 0)
BIAS = ((2, 1, HEAD_K), "w", 0)
GAIN = ((1, HEAD_V), "w", 0)
RISE = ((0, 2), (1, 3))
FALL = ((2, 0), (3, 1))


def mixer(own, pair, up, bias, gain, shift):
    steps = own.shape[0] // CHUNK
    logits, cums, starts, end = call(
        state_kernel,
        steps,
        [K, V, K, V, LOW, UP, BIAS],
        [(CUMS, F32), (CUMS, F32), ((STATES, "t", 0), F32), (STATE, F32)],
        [MEMORY],
        4 << 30,
        (own, own, pair, pair, own, up, bias),
        shift,
    )
    arrived = lax.ppermute(end[::-1], "tensor", RISE)
    gated_own, gated_pair, mixed, full = call(
        mix_kernel,
        steps,
        [Q, K, V, G, Q, K, V, G, CUMS, (STATES, "t", 0), STATE, GAIN],
        [((WIDE, "r", 0), BF), ((WIDE, "r", 0), BF), (HEADS_WIDE, F32), ((STATES, "t", 0), BF)],
        [SQUARES, PASSED],
        6 << 30,
        (own, own, own, own, pair, pair, pair, pair, cums, starts, arrived, gain),
        shift,
    )
    return gated_own, gated_pair, (logits, cums, mixed, full)


def mixer_back(own, pair, up, gain, shift, kept, d_own, d_pair):
    logits, cums, mixed, full = kept
    steps = own.shape[0] // CHUNK
    grad = (WIDE, "r", 0)
    d_mixed, d_gate, ends, first, d_gain = call(
        gate_back_kernel,
        steps,
        [Q, G, grad, Q, G, grad, CUMS, HEADS_WIDE, GAIN],
        [(HEADS_WIDE, BF), (HEADS_WIDE, BF), ((STATES, "t", 0), F32), (STATE, F32), (GAIN, F32)],
        [MEMORY],
        6 << 30,
        (own, own, d_own, pair, pair, d_pair, cums, mixed, gain),
        shift,
        backward=True,
    )
    arrived = lax.ppermute(first[::-1], "tensor", FALL)
    back_own, back_pair, d_up, d_bias = call(
        mix_back_kernel,
        steps,
        [Q, K, V, LOW, Q, K, V, CUMS, CUMS, (STATES, "t", 0), (STATES, "t", 0), STATE, UP, HEADS_WIDE, HEADS_WIDE],
        [
            (((CHUNK, own.shape[1]), "r", 0), BF),
            (((CHUNK, pair.shape[1]), "r", 0), BF),
            (UP, F32),
            (BIAS, F32),
        ],
        [pltpu.VMEM((2, CHUNK, HEAD_K), F32), pltpu.VMEM((2, CHUNK, HEAD_K), F32), SQUARES, SQUARES, PASSED],
        12 << 30,
        (own, own, own, own, pair, pair, pair, cums, logits, full, ends, arrived, up, d_mixed, d_gate),
        shift,
        backward=True,
    )
    return back_own, back_pair, d_up, d_bias, d_gain


def hidden_kernel(rows, cot, *refs):
    for h in range(2):
        gate_w, up_w, down_w = refs[3 * h : 3 * h + 3]
        hidden, d_gate, d_up = refs[6 + 3 * h : 9 + 3 * h]
        gate = project(rows[...], gate_w[...])
        up = project(rows[...], up_w[...])
        grad = project(cot[...], down_w[...])
        sigmoid = jax.nn.sigmoid(gate)
        silu = gate * sigmoid
        hidden[...] = (silu * up).astype(BF)
        d_up[...] = (grad * silu).astype(BF)
        d_gate[...] = (grad * up * sigmoid * (1.0 + gate * (1.0 - sigmoid))).astype(BF)


def hidden_products(rows, cot, weights):
    tokens, width = rows.shape
    units = weights[0].shape[1]
    tile = min(FF_ROWS, tokens)
    by_row = pl.BlockSpec((tile, width), lambda n: (n, 0))
    fixed = pl.BlockSpec((width, units), lambda n: (0, 0))
    return pl.pallas_call(
        hidden_kernel,
        grid=(tokens // tile,),
        in_specs=[by_row, by_row] + [fixed] * 6,
        out_specs=[pl.BlockSpec((tile, units), lambda n: (n, 0))] * 6,
        out_shape=[jax.ShapeDtypeStruct((tokens, units), BF)] * 6,
        compiler_params=pltpu.CompilerParams(vmem_limit_bytes=56 << 20),
        cost_estimate=pl.CostEstimate(
            flops=12 * tokens * width * units, bytes_accessed=24 << 20, transcendentals=0
        ),
    )(rows, cot, *weights)


def norm_back(grad_out, normal, scale, gain):
    scaled_grad = grad_out * gain
    return scale * (scaled_grad - normal * jnp.mean(scaled_grad * normal, axis=-1, keepdims=True))


def sum_cores(full):
    half = full.shape[0] // 2
    return full[:half].astype(F32) + swap(full[half:].astype(BF), "tensor", CORE).astype(F32)


def both_cores(mine):
    return jnp.concatenate([mine, swap(mine, "tensor", CORE)], axis=0)


def local(
    tokens,
    norm_gain,
    query_weight,
    key_weight,
    value_weight,
    gate_weight,
    low_down,
    low_up,
    rank_bias,
    head_gain,
    out_weight,
    mlp_gain,
    mlp_gate,
    mlp_up,
    mlp_down,
    cotangent,
):
    count = lax.axis_size("dp")
    rows, rank = low_down.shape
    width = rows * count
    member = lax.axis_index("tensor")
    shift = (member % 2 * (tokens.shape[0] // CHUNK)).astype(jnp.int32).reshape(1)

    def tall(array):
        return jnp.pad(array, ((0, rows - array.shape[0]), (0, 0)))

    small = [low_down, norm_gain[:, None], mlp_gain[:, None], tall(low_up[0].T), tall(rank_bias.T), tall(head_gain[:, None])]
    small = jnp.concatenate(small, axis=1)
    small = jnp.pad(small, ((0, 0), (0, LANES - small.shape[1])))
    in_own, in_pair = gather(jnp.concatenate([query_weight, key_weight, value_weight, gate_weight, small], axis=1))
    out_own, out_pair = gather(out_weight.T)
    gate_own, gate_pair = gather(mlp_gate)
    up_own, up_pair = gather(mlp_up)
    down_own, down_pair = gather(mlp_down.T)

    def joined(pieces, start=0, stop=None):
        return jnp.concatenate([p[:, start:stop] for p in pieces], axis=0)

    used = 2 * HEAD_K + 2 * HEAD_V
    w_in_own = joined(in_own)
    w_in_pair = joined(in_pair, 0, used)
    small_own = w_in_own[:, used:]
    small_pair = joined(in_pair, used)
    w_out_own, w_out_pair = joined(out_own), joined(out_pair)
    w_gate_own, w_gate_pair = joined(gate_own), joined(gate_pair)
    w_up_own, w_up_pair = joined(up_own), joined(up_pair)
    w_down_own, w_down_pair = joined(down_own), joined(down_pair)

    order = block_matrix()

    def to_actual(array, start, stop, depth):
        blocks = array[:, start:stop].reshape(count, rows, stop - start)[:, :depth].astype(F32)
        flat = exact(order, blocks.reshape(count, depth * (stop - start)))
        return flat.reshape(count * depth, stop - start)

    def to_places(array, depth):
        blocks = array.reshape(count, depth, array.shape[1])
        flat = lax.dot_general(
            order, blocks.reshape(count, -1), (((0,), (0,)), ((), ())), preferred_element_type=F32, precision=TOP_PRECISION
        )
        return flat.reshape(count, depth, array.shape[1])

    slots = rank + 2
    gain_one = small_own[:, rank].astype(F32)
    gain_two = small_own[:, rank + 1].astype(F32)
    deep = low_up.shape[2]
    up, bias = [], []
    for array in (small_own, small_pair):
        head = to_actual(array, slots, slots + rank + 1, deep)
        up.append(jnp.pad(head[:, :rank].T, ((0, LANES - rank), (0, 0))))
        bias.append(head[:, rank][None, :])
    up, bias = jnp.stack(up), jnp.stack(bias)
    gain_head = to_actual(small_own, slots + rank + 1, slots + rank + 2, head_gain.shape[0]).reshape(1, -1)

    places = place_matrix(width)
    tokens = project(tokens, places).astype(BF)
    cot_mine = project(cotangent, places).astype(BF)
    cot_rows = both_cores(cot_mine)

    inputs = tokens.astype(F32)
    scale_one = lax.rsqrt(jnp.mean(inputs * inputs, axis=-1, keepdims=True) + NORM_EPS)
    normal_one = inputs * scale_one
    normed_rows = both_cores((normal_one * gain_one).astype(BF))
    proj_own = project(normed_rows, w_in_own)
    proj_pair = project(normed_rows, w_in_pair)
    gated_own, gated_pair, kept = mixer(proj_own, proj_pair, up, bias, gain_head, shift)
    middle = inputs + sum_cores(contract_last(gated_own, w_out_own) + contract_last(gated_pair, w_out_pair))
    scale_two = lax.rsqrt(jnp.mean(middle * middle, axis=-1, keepdims=True) + NORM_EPS)
    normal_two = middle * scale_two
    mlp_rows = both_cores((normal_two * gain_two).astype(BF))

    hidden_own, d_gate_own, d_up_own, hidden_pair, d_gate_pair, d_up_pair = hidden_products(
        mlp_rows, cot_rows, (w_gate_own, w_up_own, w_down_own, w_gate_pair, w_up_pair, w_down_pair)
    )
    grad_second = sum_cores(
        contract_last(d_gate_own, w_gate_own)
        + contract_last(d_gate_pair, w_gate_pair)
        + contract_last(d_up_own, w_up_own)
        + contract_last(d_up_pair, w_up_pair)
    )
    outputs = middle + sum_cores(contract_last(hidden_own, w_down_own) + contract_last(hidden_pair, w_down_pair))
    block_out = contract_last(outputs.astype(BF), places).astype(BF)

    def weight_grad(left, own, pair):
        return scatter(contract_rows(left, own).astype(BF), contract_rows(left, pair).astype(BF))

    grad_mlp_down = weight_grad(cot_rows, hidden_own, hidden_pair).T
    grad_mlp_gate = weight_grad(mlp_rows, d_gate_own, d_gate_pair)
    grad_mlp_up = weight_grad(mlp_rows, d_up_own, d_up_pair)

    grad_mlp_gain = jnp.sum(grad_second * normal_two, axis=0)
    grad_middle = cot_mine.astype(F32) + norm_back(grad_second, normal_two, scale_two, gain_two)
    mixer_cot = both_cores(grad_middle.astype(BF))
    grad_out_weight = weight_grad(mixer_cot, gated_own, gated_pair).T
    back_own, back_pair, d_up, d_bias, d_gain = mixer_back(
        proj_own, proj_pair, up, gain_head, shift, kept, project(mixer_cot, w_out_own), project(mixer_cot, w_out_pair)
    )
    grad_normed = sum_cores(contract_last(back_own, w_in_own) + contract_last(back_pair, w_in_pair))
    grad_norm_gain = jnp.sum(grad_normed * normal_one, axis=0)
    grad_inputs = grad_middle + norm_back(grad_normed, normal_one, scale_one, gain_one)
    high = grad_inputs.astype(BF)
    rest = (grad_inputs - high.astype(F32)).astype(BF)
    grad_inputs = contract_last(high, places) + contract_last(rest, places)

    grad_own = contract_rows(normed_rows, back_own).astype(BF)
    grad_pair = contract_rows(normed_rows, back_pair).astype(BF)
    grad_in = scatter(grad_own[:, :used], grad_pair)

    quarter = rows // 4
    shared = jnp.concatenate(
        [
            grad_own[:, used : used + rank].astype(F32),
            grad_norm_gain[:, None],
            grad_mlp_gain[:, None],
            jnp.pad(
                to_places(d_gain.reshape(-1, 1), head_gain.shape[0]).reshape(count, 4, -1, 1),
                ((0, 0), (0, 0), (0, quarter - head_gain.shape[0] // 4), (0, 0)),
            ).reshape(width, 1),
        ],
        axis=1,
    )
    half_of = lax.broadcasted_iota(jnp.int32, (width, 1), 0) % rows // (2 * quarter)
    pieces = []
    for h, half in ((0, member // 2), (1, 1 - member // 2)):
        head = jnp.concatenate([d_up[h, :rank].T, d_bias[h].T], axis=1)
        head = jnp.pad(to_places(head, deep), ((0, 0), (0, rows - deep), (0, 0))).reshape(width, rank + 1)
        piece = jnp.concatenate([jnp.where(half_of == half, shared, 0.0), head], axis=1)
        pieces.append(jnp.pad(piece, ((0, 0), (0, LANES - piece.shape[1]))).astype(BF))
    small_grad = scatter(*pieces)
    grad_low_up = small_grad[:deep, rank + 3 : 2 * rank + 3].T[None]
    grad_rank_bias = small_grad[:deep, 2 * rank + 3][None]
    shared = small_grad + swap(small_grad.astype(BF), "tensor", CORE).astype(F32)
    shared = lax.dynamic_slice_in_dim(shared, member * quarter, quarter, 0)

    return (
        block_out,
        grad_inputs,
        shared[:, rank],
        grad_in[:, :HEAD_K],
        grad_in[:, HEAD_K : 2 * HEAD_K],
        grad_in[:, 2 * HEAD_K : 2 * HEAD_K + HEAD_V],
        grad_in[:, 2 * HEAD_K + HEAD_V :],
        shared[:, :rank],
        grad_low_up,
        grad_rank_bias,
        shared[: head_gain.shape[0] // 4, rank + 2],
        grad_out_weight,
        shared[:, rank + 1],
        grad_mlp_gate,
        grad_mlp_up,
        grad_mlp_down,
    )


def solution(mesh):
    return jax.shard_map(
        local,
        mesh=mesh,
        in_specs=(
            P(("dp", "tensor"), None),
            P("dp"),
            P("dp", "tensor"),
            P("dp", "tensor"),
            P("dp", "tensor"),
            P("dp", "tensor"),
            P("dp", None),
            P("tensor", None, "dp"),
            P("tensor", "dp"),
            P("dp"),
            P("tensor", "dp"),
            P("dp"),
            P("dp", "tensor"),
            P("dp", "tensor"),
            P("tensor", "dp"),
            P(("dp", "tensor"), None),
        ),
        out_specs=(
            P(("dp", "tensor"), None),
            P(("dp", "tensor"), None),
            P(("dp", "tensor")),
            P("dp", "tensor"),
            P("dp", "tensor"),
            P("dp", "tensor"),
            P("dp", "tensor"),
            P(("dp", "tensor"), None),
            P("tensor", None, "dp"),
            P("tensor", "dp"),
            P(("dp", "tensor")),
            P("tensor", "dp"),
            P(("dp", "tensor")),
            P("dp", "tensor"),
            P("dp", "tensor"),
            P("tensor", "dp"),
        ),
        check_vma=False,
    )
```

```python
import jax
import jax.numpy as jnp
from jax import lax
from jax.experimental import pallas as pl
from jax.experimental.pallas import tpu as pltpu
from jax.sharding import PartitionSpec as P

HEAD_K = 128
HEAD_V = 256
CHUNK = 128
TILE = 256
LANES = 128
SAFE_RANGE = 60.0

TOP_PRECISION = lax.Precision.HIGHEST
NORM_EPS = 1e-06
HEAD_EPS = 1e-05
NORMALIZER = 16.0
CORE = 1
PAIR = 2
BF = jnp.bfloat16
F32 = jnp.float32


def swap(array, axis, mask):
    size = lax.axis_size(axis)
    return lax.ppermute(array, axis, [(i, i ^ mask) for i in range(size)])


def after(array, *others):
    return lax.optimization_barrier((array, *others))[0]


def slow_masks():
    mask, result = lax.axis_size("dp") // 2, []
    while mask > 1:
        result.append(mask)
        mask //= 2
    return result


def gather_slow(part):
    for mask in slow_masks():
        part = jnp.concatenate([part, swap(part, "dp", mask)], axis=0)
    return part


def gather_fast(held):
    half = held.shape[0] // 2
    beside = swap(held, "dp", 1)
    pair = swap(held, "tensor", PAIR)
    pair_low = swap(pair[:half], "dp", 1)
    pair_high = swap(beside[half:], "tensor", PAIR)
    return held, beside, pair, pair_low, pair_high


def send_first(own, pair):
    low = swap(pair[2], "dp", 1)
    high = swap(pair[3], "tensor", PAIR)
    beside_low = swap(own[2], "dp", 1)
    pair_rest = swap(pair[1], "tensor", PAIR)
    return low, high, beside_low, pair_rest


def send_second(own, pair, first, *others):
    low, high, beside_low, pair_rest = first
    if others:
        low, high = after(low, *others), after(high, *others)
    beside_high = swap((own[3].astype(F32) + high.astype(F32)).astype(BF), "dp", 1)
    pair_sum = swap((pair[0].astype(F32) + low.astype(F32)).astype(BF), "tensor", PAIR)
    return [
        own[0].astype(F32) + beside_low.astype(F32) + pair_sum.astype(F32),
        own[1].astype(F32) + beside_high.astype(F32) + pair_rest.astype(F32),
    ]


def send_slow(kept, given, mask):
    return kept + swap(given.astype(BF), "dp", mask).astype(F32)


def scatter_slow(halves, *others):
    total, given = halves
    if others:
        given = after(given, *others)
    masks = slow_masks()[::-1]
    total = send_slow(total, given, masks[0])
    for mask in masks[1:]:
        rows = total.shape[0] // 2
        total = send_slow(total[:rows], total[rows:], mask)
    return total


def slot_owner(slot):
    count = lax.axis_size("dp")
    bits = count.bit_length() - 1
    delta = sum(((slot >> i) & 1) << (bits - 1 - i) for i in range(bits))
    return delta ^ lax.axis_index("dp")


def place_matrix(width):
    block = width // lax.axis_size("dp")
    feature = lax.broadcasted_iota(jnp.int32, (width, width), 0)
    place = lax.broadcasted_iota(jnp.int32, (width, width), 1)
    return (feature == slot_owner(place // block) * block + place % block).astype(BF)


def small_places(width, length, groups):
    count = lax.axis_size("dp")
    block, deep = width // count, length // count
    place = lax.broadcasted_iota(jnp.int32, (width, length), 0)
    entry = lax.broadcasted_iota(jnp.int32, (width, length), 1)
    inside, room = place % block, block // groups
    held = inside % room < deep // groups
    stands = slot_owner(place // block) * deep + inside // room * (deep // groups) + inside % room
    return (held & (entry == stands)).astype(BF)


def contract_rows(former, latter):
    return lax.dot_general(former, latter, (((0,), (0,)), ((), ())), preferred_element_type=F32)


def contract_last(former, latter):
    return lax.dot_general(former, latter, (((1,), (1,)), ((), ())), preferred_element_type=F32)


def project(former, latter):
    return jnp.dot(former, latter, preferred_element_type=F32)


def exact(former, latter):
    return jnp.dot(former, latter, preferred_element_type=F32, precision=TOP_PRECISION)


def positions():
    row = lax.broadcasted_iota(jnp.int32, (CHUNK, CHUNK), 0)
    col = lax.broadcasted_iota(jnp.int32, (CHUNK, CHUNK), 1)
    return row, col


def level_terms(cum, size):
    row, col = positions()
    boundary = row // (2 * size) * (2 * size) + size - 1
    at_boundary = exact((col == boundary).astype(F32), cum)
    fade = jnp.exp(-jnp.abs(cum - at_boundary))
    same = row // (2 * size) == col // (2 * size)
    mask = same & (row % (2 * size) >= size) & (col % (2 * size) < size)
    return fade, mask


def state_kernel(shift, k_own, v_own, k_pair, v_pair, low, up, bias, logits, cums, starts, end, memory):
    n = pl.program_id(0)

    @pl.when(n == 0)
    def _():
        memory[...] = jnp.zeros_like(memory)

    row, col = positions()
    triangle = (row >= col).astype(F32)
    for h, (k_ref, v_ref) in enumerate(((k_own, v_own), (k_pair, v_pair))):
        columns = slice(h * HEAD_K, (h + 1) * HEAD_K)
        logit = exact(low[...], up[h]) + bias[h]
        decay = (jnp.minimum(logit, 0.0) - jnp.log1p(jnp.exp(-jnp.abs(logit)))) / NORMALIZER
        cum = exact(triangle, decay)
        closing = cum[CHUNK - 1 :, :]
        logits[:, columns] = logit
        cums[:, columns] = cum
        starts[0, h] = memory[h]
        faded = (k_ref[...].astype(BF).astype(F32) * jnp.exp(closing - cum)).astype(BF)
        memory[h] = jnp.exp(closing) * memory[h] + contract_rows(v_ref[...].astype(BF), faded)

    @pl.when(n == pl.num_programs(0) - 1)
    def _():
        end[...] = memory[...]


def mix_kernel(
    shift, q_own, k_own, v_own, g_own, q_pair, k_pair, v_pair, g_pair, cums, starts, arrived, gain,
    gated_own, gated_pair, mixed_out, full, scores, passed,
):
    n = pl.program_id(0)

    @pl.when(n == 0)
    def _():
        passed[...] = jnp.zeros_like(passed)

    row, col = positions()
    heads = ((q_own, k_own, v_own, g_own, gated_own), (q_pair, k_pair, v_pair, g_pair, gated_pair))
    lowest = jnp.min(cums[CHUNK - 1 :, :])

    @pl.when(lowest > -SAFE_RANGE)
    def _():
        for h, (q_ref, k_ref, _, _, _) in enumerate(heads):
            cum = cums[:, h * HEAD_K : (h + 1) * HEAD_K]
            middle = cum[CHUNK // 2 : CHUNK // 2 + 1, :]
            q = q_ref[...].astype(BF).astype(F32)
            k = k_ref[...].astype(BF).astype(F32)
            both = contract_last((q * jnp.exp(cum - middle)).astype(BF), (k * jnp.exp(middle - cum)).astype(BF))
            scores[h] = jnp.where(row >= col, both, 0.0)

    @pl.when(lowest <= -SAFE_RANGE)
    def _():
        for h, (q_ref, k_ref, _, _, _) in enumerate(heads):
            cum = cums[:, h * HEAD_K : (h + 1) * HEAD_K]
            q = q_ref[...].astype(BF).astype(F32)
            k = k_ref[...].astype(BF).astype(F32)
            scores[h] = jnp.where(row == col, jnp.sum(q * k, axis=1, keepdims=True), 0.0)

            def level(step, carry):
                fade, mask = level_terms(cum, jnp.int32(1) << step)
                both = contract_last((q * fade).astype(BF), (k * fade).astype(BF))
                scores[h] = scores[h] + jnp.where(mask, both, 0.0)
                return carry

            lax.fori_loop(0, CHUNK.bit_length() - 1, level, 0)

    for h, (q_ref, _, v_ref, g_ref, out) in enumerate(heads):
        cum = cums[:, h * HEAD_K : (h + 1) * HEAD_K]
        state = (starts[0, h] + jnp.exp(passed[h]) * arrived[h].astype(F32)).astype(BF)
        full[0, h] = state
        passed[h] = passed[h] + cum[CHUNK - 1 :, :]
        q = q_ref[...].astype(BF).astype(F32)
        mixed = project(scores[h].astype(BF), v_ref[...].astype(BF))
        mixed = mixed + contract_last((q * jnp.exp(cum)).astype(BF), state)
        mixed = mixed * HEAD_K**-0.5
        mixed_out[:, h * HEAD_V : (h + 1) * HEAD_V] = mixed
        scale = lax.rsqrt(jnp.mean(mixed * mixed, axis=-1, keepdims=True) + HEAD_EPS)
        g = g_ref[...]
        out[...] = (mixed * scale * gain[...] * g * jax.nn.sigmoid(g)).astype(BF)


def gate_back_kernel(
    shift, q_own, g_own, d_own, q_pair, g_pair, d_pair, cums, mixed_in, gain,
    d_mixed, d_gate, ends, first, d_gain, memory,
):
    n = pl.program_id(0)

    @pl.when(n == 0)
    def _():
        memory[...] = jnp.zeros_like(memory)
        d_gain[...] = jnp.zeros_like(d_gain)

    for h, (q_ref, g_ref, d_ref) in enumerate(((q_own, g_own, d_own), (q_pair, g_pair, d_pair))):
        wide = slice(h * HEAD_V, (h + 1) * HEAD_V)
        cum = cums[:, h * HEAD_K : (h + 1) * HEAD_K]
        mixed = mixed_in[:, wide]
        scale = lax.rsqrt(jnp.mean(mixed * mixed, axis=-1, keepdims=True) + HEAD_EPS)
        normal = mixed * scale
        g, grad = g_ref[...], d_ref[...]
        sigmoid = jax.nn.sigmoid(g)
        silu = g * sigmoid
        d_gain[...] += jnp.sum(grad * normal * silu, axis=0, keepdims=True)
        scaled = grad * gain[...]
        d_gate[:, wide] = (scaled * normal * sigmoid * (1.0 + g * (1.0 - sigmoid))).astype(BF)
        scaled = scaled * silu
        back = scale * (scaled - normal * jnp.mean(scaled * normal, axis=-1, keepdims=True))
        back = (back * HEAD_K**-0.5).astype(BF)
        d_mixed[:, wide] = back
        ends[0, h] = memory[h]
        q = q_ref[...].astype(BF).astype(F32)
        faded = (q * jnp.exp(cum)).astype(BF)
        memory[h] = jnp.exp(cum[CHUNK - 1 :, :]) * memory[h] + contract_rows(back, faded)

    @pl.when(n == pl.num_programs(0) - 1)
    def _():
        first[...] = memory[...]


def mix_back_kernel(
    shift, q_own, k_own, v_own, low, q_pair, k_pair, v_pair, cums, logits, full, ends, arrived, up,
    d_mixed, d_gate, back_own, back_pair, d_up, d_bias, d_q, d_k, d_cum, scores, grads, passed,
):
    n = pl.program_id(0)

    @pl.when(n == 0)
    def _():
        passed[...] = jnp.zeros_like(passed)
        d_up[...] = jnp.zeros_like(d_up)
        d_bias[...] = jnp.zeros_like(d_bias)

    row, col = positions()
    heads = ((q_own, k_own, v_own, back_own), (q_pair, k_pair, v_pair, back_pair))
    lowest = jnp.min(cums[CHUNK - 1 :, :])
    for h, (_, _, v_ref, _) in enumerate(heads):
        back = d_mixed[:, h * HEAD_V : (h + 1) * HEAD_V]
        grads[h] = contract_last(back, v_ref[...].astype(BF))

    @pl.when(lowest > -SAFE_RANGE)
    def _():
        for h, (q_ref, k_ref, _, _) in enumerate(heads):
            cum = cums[:, h * HEAD_K : (h + 1) * HEAD_K]
            middle = cum[CHUNK // 2 : CHUNK // 2 + 1, :]
            q = q_ref[...].astype(BF).astype(F32)
            k = k_ref[...].astype(BF).astype(F32)
            rise, fall = jnp.exp(cum - middle), jnp.exp(middle - cum)
            q_faded, k_faded = (q * rise).astype(BF), (k * fall).astype(BF)
            scores[h] = jnp.where(row >= col, contract_last(q_faded, k_faded), 0.0)
            strict = jnp.where(row > col, grads[h], 0.0).astype(BF)
            q_part, k_part = project(strict, k_faded), contract_rows(strict, q_faded)
            d_q[h], d_k[h] = q_part * rise, k_part * fall
            d_cum[h] = q_faded.astype(F32) * q_part - k_faded.astype(F32) * k_part

    @pl.when(lowest <= -SAFE_RANGE)
    def _():
        for h, (q_ref, k_ref, _, _) in enumerate(heads):
            cum = cums[:, h * HEAD_K : (h + 1) * HEAD_K]
            q = q_ref[...].astype(BF).astype(F32)
            k = k_ref[...].astype(BF).astype(F32)
            scores[h] = jnp.where(row == col, jnp.sum(q * k, axis=1, keepdims=True), 0.0)
            d_q[h] = jnp.zeros((CHUNK, HEAD_K), F32)
            d_k[h] = jnp.zeros((CHUNK, HEAD_K), F32)
            d_cum[h] = jnp.zeros((CHUNK, HEAD_K), F32)

            def level(step, carry):
                fade, mask = level_terms(cum, jnp.int32(1) << step)
                q_faded, k_faded = (q * fade).astype(BF), (k * fade).astype(BF)
                scores[h] = scores[h] + jnp.where(mask, contract_last(q_faded, k_faded), 0.0)
                crossing = jnp.where(mask, grads[h], 0.0).astype(BF)
                q_part, k_part = project(crossing, k_faded), contract_rows(crossing, q_faded)
                d_q[h] = d_q[h] + q_part * fade
                d_k[h] = d_k[h] + k_part * fade
                d_cum[h] = d_cum[h] + q_faded.astype(F32) * q_part - k_faded.astype(F32) * k_part
                return carry

            lax.fori_loop(0, CHUNK.bit_length() - 1, level, 0)

    later = (row <= col).astype(F32)
    d_low = jnp.zeros((CHUNK, LANES), F32)
    for h, (q_ref, k_ref, v_ref, out) in enumerate(heads):
        columns = slice(h * HEAD_K, (h + 1) * HEAD_K)
        wide = slice(h * HEAD_V, (h + 1) * HEAD_V)
        cum = cums[:, columns]
        closing = cum[CHUNK - 1 :, :]
        q = q_ref[...].astype(BF).astype(F32)
        k = k_ref[...].astype(BF).astype(F32)
        v, back, state = v_ref[...].astype(BF), d_mixed[:, wide], full[0, h]
        state_grad = ends[0, h] + jnp.exp(passed[h]) * arrived[h].astype(F32)
        passed[h] = passed[h] + closing
        low_grad = state_grad.astype(BF)
        fade = jnp.exp(closing - cum)
        q_state = project(back, state) * jnp.exp(cum)
        k_state = project(v, low_grad) * fade
        diagonal = jnp.sum(jnp.where(row == col, grads[h], 0.0), axis=1, keepdims=True)
        d_v = contract_rows(scores[h].astype(BF), back) + contract_last((k * fade).astype(BF), low_grad)
        d_closing = jnp.sum(k * k_state, axis=0, keepdims=True) + jnp.exp(closing) * jnp.sum(
            state.astype(F32) * state_grad, axis=0, keepdims=True
        )
        d_decay = exact(later, d_cum[h] + q * q_state - k * k_state) + d_closing
        d_logit = d_decay * (jax.nn.sigmoid(-logits[:, columns]) / NORMALIZER)
        out[:, :HEAD_K] = (d_q[h] + q_state + diagonal * k).astype(BF)
        out[:, HEAD_K : 2 * HEAD_K] = (d_k[h] + k_state + diagonal * q).astype(BF)
        out[:, 2 * HEAD_K : 2 * HEAD_K + HEAD_V] = d_v.astype(BF)
        out[:, 2 * HEAD_K + HEAD_V : 2 * HEAD_K + 2 * HEAD_V] = d_gate[:, wide]
        low_logit = d_logit.astype(BF)
        d_low = d_low + contract_last(low_logit, up[h].astype(BF))
        d_up[h] = d_up[h] + contract_rows(low[...].astype(BF), low_logit)
        d_bias[h] = d_bias[h] + jnp.sum(d_logit, axis=0, keepdims=True)
    back_own[:, 2 * HEAD_K + 2 * HEAD_V :] = d_low.astype(BF)


def whole(shape):
    return pl.BlockSpec(shape, lambda n, shift: (0,) * len(shape))


def call(kernel, steps, ins, outs, scratch, flops, arrays, shift, backward=False):
    def at(n):
        return steps - 1 - n if backward else n

    def spec(entry):
        shape, kind, column = entry
        if kind == "r":
            return pl.BlockSpec(shape, lambda n, shift: ((at(n) + shift[0]) % steps, column))
        if kind == "t":
            return pl.BlockSpec(shape, lambda n, shift: (at(n),) + (0,) * (len(shape) - 1))
        return whole(shape)

    shapes = []
    for (shape, kind, _), dtype in outs:
        shapes.append(jax.ShapeDtypeStruct((shape[0] * (steps if kind != "w" else 1),) + shape[1:], dtype))
    return pl.pallas_call(
        kernel,
        grid_spec=pltpu.PrefetchScalarGridSpec(
            num_scalar_prefetch=1,
            grid=(steps,),
            in_specs=[spec(entry) for entry in ins],
            out_specs=[spec(entry) for entry, _ in outs],
            scratch_shapes=scratch,
        ),
        out_shape=shapes,
        compiler_params=pltpu.CompilerParams(vmem_limit_bytes=40 << 20),
        cost_estimate=pl.CostEstimate(flops=flops, bytes_accessed=12 << 20, transcendentals=0),
    )(shift, *arrays)


NARROW, WIDE = (CHUNK, HEAD_K), (CHUNK, HEAD_V)
STATES = (1, 2, HEAD_V, HEAD_K)
Q, K, V, G = (NARROW, "r", 0), (NARROW, "r", 1), (WIDE, "r", 1), (WIDE, "r", 2)
LOW = (NARROW, "r", (2 * HEAD_K + 2 * HEAD_V) // LANES)
CUMS = ((CHUNK, 2 * HEAD_K), "t", 0)
HEADS_WIDE = ((CHUNK, 2 * HEAD_V), "t", 0)
STATE = ((2, HEAD_V, HEAD_K), "w", 0)
SQUARES = pltpu.VMEM((2, CHUNK, CHUNK), F32)
NARROWS = pltpu.VMEM((2, CHUNK, HEAD_K), F32)
MEMORY = pltpu.VMEM((2, HEAD_V, HEAD_K), F32)
PASSED = pltpu.VMEM((2, 1, HEAD_K), F32)
UP = ((2, LANES, HEAD_K), "w", 0)
BIAS = ((2, 1, HEAD_K), "w", 0)
GAIN = ((1, HEAD_V), "w", 0)
RISE = ((0, 2), (1, 3))
FALL = ((2, 0), (3, 1))


def mixer(own, pair, up, bias, gain, shift):
    steps = own.shape[0] // CHUNK
    logits, cums, starts, end = call(
        state_kernel,
        steps,
        [K, V, K, V, LOW, UP, BIAS],
        [(CUMS, F32), (CUMS, F32), ((STATES, "t", 0), F32), (STATE, F32)],
        [MEMORY],
        4 << 30,
        (own, own, pair, pair, own, up, bias),
        shift,
    )
    arrived = lax.ppermute(end[::-1].astype(BF), "tensor", RISE)
    gated_own, gated_pair, mixed, full = call(
        mix_kernel,
        steps,
        [Q, K, V, G, Q, K, V, G, CUMS, (STATES, "t", 0), STATE, GAIN],
        [((WIDE, "r", 0), BF), ((WIDE, "r", 0), BF), (HEADS_WIDE, F32), ((STATES, "t", 0), BF)],
        [SQUARES, PASSED],
        6 << 30,
        (own, own, own, own, pair, pair, pair, pair, cums, starts, arrived, gain),
        shift,
    )
    return gated_own, gated_pair, (logits, cums, mixed, full)


def mixer_back(own, pair, up, gain, shift, kept, d_own, d_pair):
    logits, cums, mixed, full = kept
    steps = own.shape[0] // CHUNK
    grad = (WIDE, "r", 0)
    d_mixed, d_gate, ends, first, d_gain = call(
        gate_back_kernel,
        steps,
        [Q, G, grad, Q, G, grad, CUMS, HEADS_WIDE, GAIN],
        [(HEADS_WIDE, BF), (HEADS_WIDE, BF), ((STATES, "t", 0), F32), (STATE, F32), (GAIN, F32)],
        [MEMORY],
        6 << 30,
        (own, own, d_own, pair, pair, d_pair, cums, mixed, gain),
        shift,
        backward=True,
    )
    arrived = lax.ppermute(first[::-1].astype(BF), "tensor", FALL)
    back_own, back_pair, d_up, d_bias = call(
        mix_back_kernel,
        steps,
        [Q, K, V, LOW, Q, K, V, CUMS, CUMS, (STATES, "t", 0), (STATES, "t", 0), STATE, UP, HEADS_WIDE, HEADS_WIDE],
        [
            (((CHUNK, own.shape[1]), "r", 0), BF),
            (((CHUNK, pair.shape[1]), "r", 0), BF),
            (UP, F32),
            (BIAS, F32),
        ],
        [NARROWS, NARROWS, NARROWS, SQUARES, SQUARES, PASSED],
        12 << 30,
        (own, own, own, own, pair, pair, pair, cums, logits, full, ends, arrived, up, d_mixed, d_gate),
        shift,
        backward=True,
    )
    return back_own, back_pair, d_up, d_bias, d_gain, (d_gain, d_bias)


def matmul_call(kernel, steps, ins, outs, arrays, flops):
    return pl.pallas_call(
        kernel,
        grid=(steps,),
        in_specs=[pl.BlockSpec(shape, index) for shape, index in ins],
        out_specs=[pl.BlockSpec(shape, index) for (shape, index), _ in outs],
        out_shape=[shape for _, shape in outs],
        compiler_params=pltpu.CompilerParams(vmem_limit_bytes=56 << 20),
        cost_estimate=pl.CostEstimate(flops=flops, bytes_accessed=16 << 20, transcendentals=0),
    )(*arrays)


def fixed(array):
    return array.shape, lambda n: (0,) * array.ndim


def by_rows(rows, array, start=0):
    return (rows,) + array.shape[1:], lambda n: (n + start, 0)


def struct(rows, columns, kind):
    return jax.ShapeDtypeStruct((rows, columns), kind)


def split_rows(x):
    half, quarter = x.shape[1] // 2, x.shape[1] // 4
    return x[:, :half], x[:, half : half + quarter], x[:, half + quarter :]


def own_product(x, pieces, start, stop):
    half = x.shape[1] // 2
    return project(x[:, :half], pieces[0][:, start:stop]) + project(x[:, half:], pieces[1][:, start:stop])


def pair_product(x, pieces, start, stop):
    first, second, third = split_rows(x)
    return (
        project(first, pieces[2][:, start:stop])
        + project(second, pieces[3][:, start:stop])
        + project(third, pieces[4][:, start:stop])
    )


def project_in(rows, pieces, used):
    tokens = rows.shape[0]
    columns = pieces[0].shape[1]
    tile = min(TILE, tokens)

    def kernel(x_ref, *refs):
        own, pair = refs[5:]
        x = x_ref[...]
        own[...] = own_product(x, refs, 0, columns)
        pair[...] = pair_product(x, refs, 0, used)

    outs = [struct(tokens, columns, F32), struct(tokens, used, F32)]
    return matmul_call(
        kernel,
        tokens // tile,
        [by_rows(tile, rows)] + [fixed(p) for p in pieces],
        [(by_rows(tile, o), o) for o in outs],
        (rows, *pieces),
        4 * tokens * rows.shape[1] * columns,
    )


def project_out(own, pair, pieces, start, kind, part):
    tokens, width = own.shape[0] // 2, 2 * pieces[0].shape[0]
    tile = min(TILE, tokens)
    half, quarter = width // 2, width // 4
    own_stop, pair_stop = start + own.shape[1], start + pair.shape[1]

    def kernel(own_ref, pair_ref, a, b, c, d, e, out):
        mine, other = own_ref[...], pair_ref[...]
        out[:, :half] = (
            contract_last(mine, a[:, start:own_stop]) + contract_last(other, c[:, start:pair_stop])
        ).astype(kind)
        out[:, half : half + quarter] = (
            contract_last(mine, b[:quarter, start:own_stop]) + contract_last(other, d[:, start:pair_stop])
        ).astype(kind)
        out[:, half + quarter :] = (
            contract_last(mine, b[quarter:, start:own_stop]) + contract_last(other, e[:, start:pair_stop])
        ).astype(kind)

    steps = tokens // tile
    out = struct(tokens, width, kind)
    return matmul_call(
        kernel,
        steps,
        [by_rows(tile, own, part * steps), by_rows(tile, pair, part * steps)] + [fixed(p) for p in pieces],
        [(by_rows(tile, out), out)],
        (own, pair, *pieces),
        4 * tokens * width * own.shape[1],
    )[0]


def hidden_products(rows, cot, pieces, down, start):
    tokens, width = rows.shape
    units = pieces[0].shape[1] // 2
    tile = min(TILE, tokens)

    def kernel(x_ref, c_ref, *refs):
        both, downs, outs = refs[:5], refs[5:10], refs[10:]
        x, c = x_ref[...], c_ref[...]
        for h, product in enumerate((own_product, pair_product)):
            hidden, back = outs[2 * h : 2 * h + 2]
            gate_up = product(x, both, 0, 2 * units)
            grad = product(c, downs, start, start + units)
            gate, up = gate_up[:, :units], gate_up[:, units:]
            sigmoid = jax.nn.sigmoid(gate)
            silu = gate * sigmoid
            hidden[...] = (silu * up).astype(BF)
            back[:, :units] = (grad * up * sigmoid * (1.0 + gate * (1.0 - sigmoid))).astype(BF)
            back[:, units:] = (grad * silu).astype(BF)

    outs = [struct(tokens, units, BF), struct(tokens, 2 * units, BF)] * 2
    return matmul_call(
        kernel,
        tokens // tile,
        [by_rows(tile, rows), by_rows(tile, cot)] + [fixed(p) for p in (*pieces, *down)],
        [(by_rows(tile, o), o) for o in outs],
        (rows, cot, *pieces, *down),
        12 * tokens * width * units,
    )


def weight_grads(rows, own, pair, pieces=None):
    tokens, width = rows.shape
    quarter = width // 4
    columns = own.shape[1]
    weights = () if pieces is None else tuple(pieces)

    def kernel(x_ref, own_ref, pair_ref, *refs):
        n = pl.program_id(0)
        outs = refs[len(weights) :]
        x = x_ref[...]
        own_grad, pair_grad = contract_rows(x, own_ref[...]), contract_rows(x, pair_ref[...])
        for j in range(4):

            @pl.when(n == j)
            def _():
                outs[j][...] = own_grad.astype(BF)
                outs[4 + j][...] = pair_grad.astype(BF)
                if weights:
                    own_weight, pair_weight = block_of(refs, j, quarter, columns)
                    total = own_grad * own_weight.astype(F32) + pair_grad * pair_weight.astype(F32)
                    total = jnp.sum(total, axis=1, keepdims=True)
                    outs[8][...] = jnp.broadcast_to(total, (quarter, LANES))

    shapes = [struct(quarter, columns, BF)] * 8
    outs = [(fixed(o), o) for o in shapes]
    if weights:
        total = struct(width, LANES, F32)
        outs.append((by_rows(quarter, total), total))
    result = matmul_call(
        kernel,
        4,
        [((tokens, quarter), lambda n: (0, n)), fixed(own), fixed(pair)] + [fixed(p) for p in weights],
        outs,
        (rows, own, pair, *weights),
        4 * tokens * width * columns,
    )
    return result[:4], result[4:8], result[8:]


def block_of(pieces, j, quarter, columns):
    a, b, c, d, e = pieces[:5]
    own = (a, b)[j // 2][j % 2 * quarter : (j % 2 + 1) * quarter, :columns]
    pair = (c[:quarter, :columns], c[quarter:, :columns], d[:, :columns], e[:, :columns])[j]
    return own, pair


NORM_COLUMN, MLP_COLUMN, HEAD_COLUMN, UP_COLUMN = 16, 17, 18, 32


def mixer_weight_grads(rows, own, pair, cot, gated_own, gated_pair, pieces, gain, mlp_total, up, bias, head, places):
    tokens, width = rows.shape
    quarter = width // 4
    used = pair.shape[1]
    out_end = used + gated_own.shape[1]
    columns = out_end + LANES
    rank = UP_COLUMN // 2

    def kernel(
        x_ref, own_ref, pair_ref, c_ref, gated_o, gated_p, a, b, c, d, e, gain_ref, mlp_ref, up_ref, bias_ref,
        head_ref, deep_ref, wide_ref, mine_ref, *outs,
    ):
        n = pl.program_id(0)
        x, cots = x_ref[...], c_ref[...]
        own_grad, pair_grad = contract_rows(x, own_ref[...]), contract_rows(x, pair_ref[...])
        own_out, pair_out = contract_rows(cots, gated_o[...]), contract_rows(cots, gated_p[...])
        column = lax.broadcasted_iota(jnp.int32, (quarter, LANES), 1)
        line = lax.broadcasted_iota(jnp.int32, (LANES, HEAD_K), 0)
        head_total = jnp.sum(wide_ref[...].astype(F32) * head_ref[...], axis=1, keepdims=True)
        heads = []
        for h in range(2):
            entries = jnp.where(line < rank, up_ref[h], jnp.where(line == rank, bias_ref[h], 0.0))
            entries = jnp.concatenate(
                [jnp.zeros((UP_COLUMN, HEAD_K), F32), entries[: LANES - UP_COLUMN]], axis=0
            ).astype(BF)
            heads.append(contract_last(deep_ref[...], entries))
        for j in range(4):

            @pl.when(n == j)
            def _():
                own_weight, pair_weight = block_of((a, b, c, d, e), j, quarter, own_ref.shape[1])
                low = own_weight[:, used:].astype(F32) * own_grad[:, used:]
                total = (
                    jnp.sum(own_grad[:, :used] * own_weight[:, :used].astype(F32), axis=1, keepdims=True)
                    + jnp.sum(pair_grad * pair_weight[:, :used].astype(F32), axis=1, keepdims=True)
                    + jnp.sum(low, axis=1, keepdims=True)
                )
                shared = own_grad[:, used:]
                shared = jnp.where(column == NORM_COLUMN, total / gain_ref[...], shared)
                shared = jnp.where(column == MLP_COLUMN, mlp_ref[...], shared)
                shared = jnp.where(column == HEAD_COLUMN, head_total, shared)
                mine = mine_ref[...] > 0.0
                for h, (grad, out) in enumerate(((own_grad, own_out), (pair_grad, pair_out))):
                    target = outs[4 * h + j]
                    target[:, :used] = grad[:, :used].astype(BF)
                    target[:, used:out_end] = out.astype(BF)
                    here = mine if h == 0 else jnp.logical_not(mine)
                    target[:, out_end:] = (jnp.where(here, shared, 0.0) + heads[h]).astype(BF)

    by_columns = ((tokens, quarter), lambda n: (0, n))

    def blocks(array):
        return by_rows(quarter, array)

    shapes = [struct(quarter, columns, BF)] * 8
    deep, wide, mine = places
    result = matmul_call(
        kernel,
        4,
        [by_columns, fixed(own), fixed(pair), by_columns, fixed(gated_own), fixed(gated_pair)]
        + [fixed(p) for p in pieces]
        + [blocks(gain), blocks(mlp_total), fixed(up), fixed(bias), fixed(head), blocks(deep), blocks(wide), blocks(mine)],
        [(fixed(o), o) for o in shapes],
        (rows, own, pair, cot, gated_own, gated_pair, *pieces, gain, mlp_total, up, bias, head, deep, wide, mine),
        4 * tokens * width * columns,
    )
    return result[:4], result[4:]


def gated_grads(rows, pieces, stop):
    tokens = rows.shape[0]
    tile = min(TILE, tokens)

    def kernel(x_ref, *refs):
        x = x_ref[...]
        refs[5][...] = own_product(x, refs, 0, stop)
        refs[6][...] = pair_product(x, refs, 0, stop)

    outs = [struct(tokens, stop, F32)] * 2
    return matmul_call(
        kernel,
        tokens // tile,
        [by_rows(tile, rows)] + [fixed(p) for p in pieces],
        [(by_rows(tile, o), o) for o in outs],
        (rows, *pieces),
        4 * tokens * rows.shape[1] * stop,
    )


def norm_back(grad_out, normal, scale, gain):
    scaled_grad = grad_out * gain
    return scale * (scaled_grad - normal * jnp.mean(scaled_grad * normal, axis=-1, keepdims=True))


def add_theirs(mine, theirs):
    return mine + swap(theirs, "tensor", CORE).astype(F32)


def both_cores(mine):
    return jnp.concatenate([mine, swap(mine, "tensor", CORE)], axis=0)


def local(
    tokens,
    norm_gain,
    query_weight,
    key_weight,
    value_weight,
    gate_weight,
    low_down,
    low_up,
    rank_bias,
    head_gain,
    out_weight,
    mlp_gain,
    mlp_gate,
    mlp_up,
    mlp_down,
    cotangent,
):
    count = lax.axis_size("dp")
    rows, rank = low_down.shape
    width = rows * count
    member = lax.axis_index("tensor")
    shift = (member % 2 * (tokens.shape[0] // CHUNK)).astype(jnp.int32).reshape(1)
    used = 2 * HEAD_K + 2 * HEAD_V

    def column_at(array, start, total):
        array = array if array.ndim == 2 else array[:, None]
        return jnp.pad(array, ((0, rows - array.shape[0]), (start, total - start - array.shape[1])))

    spaced = jnp.pad(head_gain.reshape(4, -1), ((0, 0), (0, (rows - head_gain.shape[0]) // 4))).reshape(-1)
    total = used + LANES
    mixer_part = column_at(query_weight, 0, total)
    for array, start in (
        (key_weight, HEAD_K),
        (value_weight, 2 * HEAD_K),
        (gate_weight, 2 * HEAD_K + HEAD_V),
        (low_down, used),
        (norm_gain, used + NORM_COLUMN),
        (mlp_gain, used + MLP_COLUMN),
        (spaced, used + HEAD_COLUMN),
        (low_up[0].T, used + UP_COLUMN),
        (rank_bias.T, used + UP_COLUMN + rank),
    ):
        mixer_part = mixer_part + column_at(array, start, total)
    mixer_held = gather_slow(mixer_part)
    mixer_in = gather_fast(mixer_held)
    down_held = gather_slow(after(jnp.concatenate([out_weight.T, mlp_down.T], axis=1), mixer_held))
    down = gather_fast(after(down_held, *mixer_in[3:]))
    up_held = gather_slow(after(jnp.concatenate([mlp_gate, mlp_up], axis=1), down_held))
    gate_up = gather_fast(after(up_held, *down[3:]))
    down_start = out_weight.shape[0]

    places = place_matrix(width)
    deep_places = small_places(width, HEAD_K, 1)
    wide_places = small_places(width, HEAD_V, 4)
    place = lax.broadcasted_iota(jnp.int32, (width, LANES), 0)
    mine_places = (place % rows // (rows // 2) == member // 2).astype(F32)
    tokens = project(tokens, places).astype(BF)
    cot_mine = project(cotangent, places).astype(BF)
    cot_rows = both_cores(cot_mine)

    small_own = jnp.concatenate([p[:, used:] for p in mixer_in[:2]], axis=0)
    small_pair = jnp.concatenate([p[:, used:] for p in mixer_in[2:]], axis=0)
    gain_one = small_own[:, NORM_COLUMN].astype(F32)
    gain_two = small_own[:, MLP_COLUMN].astype(F32)
    heads = jnp.stack([contract_rows(s, deep_places) for s in (small_own, small_pair)])
    up = jnp.pad(heads[:, UP_COLUMN : UP_COLUMN + rank], ((0, 0), (0, LANES - rank), (0, 0)))
    bias = heads[:, UP_COLUMN + rank : UP_COLUMN + rank + 1]
    gain_head = contract_rows(small_own[:, HEAD_COLUMN : HEAD_COLUMN + 1], wide_places)

    inputs = tokens.astype(F32)
    scale_one = lax.rsqrt(jnp.mean(inputs * inputs, axis=-1, keepdims=True) + NORM_EPS)
    normal_one = inputs * scale_one
    normed_rows = both_cores((normal_one * gain_one).astype(BF))
    proj_own, proj_pair = project_in(normed_rows, mixer_in, used)
    gated_own, gated_pair, kept = mixer(proj_own, proj_pair, up, bias, gain_head, shift)
    theirs = project_out(gated_own, gated_pair, down, 0, BF, 1)
    middle = inputs + add_theirs(project_out(gated_own, gated_pair, down, 0, F32, 0), theirs)
    scale_two = lax.rsqrt(jnp.mean(middle * middle, axis=-1, keepdims=True) + NORM_EPS)
    normal_two = middle * scale_two
    mlp_rows = both_cores((normal_two * gain_two).astype(BF))

    hidden_own, back_gu_own, hidden_pair, back_gu_pair = hidden_products(mlp_rows, cot_rows, gate_up, down, down_start)
    grad_down_own, grad_down_pair, _ = weight_grads(cot_rows, hidden_own, hidden_pair)
    down_first = send_first(grad_down_own, grad_down_pair)
    theirs = project_out(back_gu_own, back_gu_pair, gate_up, 0, BF, 1)
    grad_second = add_theirs(project_out(back_gu_own, back_gu_pair, gate_up, 0, F32, 0), theirs)
    grad_gu_own, grad_gu_pair, (mlp_total,) = weight_grads(mlp_rows, back_gu_own, back_gu_pair, gate_up)
    down_second = send_second(grad_down_own, grad_down_pair, down_first, mlp_total)
    gu_first = send_first(grad_gu_own, grad_gu_pair)
    grad_middle = cot_mine.astype(F32) + norm_back(grad_second, normal_two, scale_two, gain_two)
    mixer_cot = both_cores(grad_middle.astype(BF))

    d_own, d_pair = gated_grads(mixer_cot, down, down_start)
    back_own, back_pair, d_up, d_bias, d_gain, marks = mixer_back(
        proj_own, proj_pair, up, gain_head, shift, kept, d_own, d_pair
    )
    gu_second = send_second(grad_gu_own, grad_gu_pair, gu_first, marks[0])
    grad_mlp_down = scatter_slow(down_second, marks[0]).T
    grad_gu = scatter_slow(gu_second, marks[1])

    own_blocks, pair_blocks = mixer_weight_grads(
        normed_rows, back_own, back_pair, mixer_cot, gated_own, gated_pair, mixer_in,
        jnp.broadcast_to(gain_one[:, None], (width, LANES)), mlp_total / gain_two[:, None],
        d_up, d_bias, d_gain, (deep_places, wide_places, mine_places),
    )
    mixer_first = send_first(own_blocks, pair_blocks)
    theirs = project_out(back_own, back_pair, mixer_in, 0, BF, 1)
    grad_normed = add_theirs(project_out(back_own, back_pair, mixer_in, 0, F32, 0), theirs)
    grad_in = scatter_slow(send_second(own_blocks, pair_blocks, mixer_first))

    hidden_own = after(hidden_own, back_own)
    theirs = project_out(hidden_own, hidden_pair, down, down_start, BF, 1)
    outputs = middle + add_theirs(project_out(hidden_own, hidden_pair, down, down_start, F32, 0), theirs)
    block_out = contract_last(outputs.astype(BF), places).astype(BF)
    grad_inputs = grad_middle + norm_back(grad_normed, normal_one, scale_one, gain_one)
    high = grad_inputs.astype(BF)
    rest = (grad_inputs - high.astype(F32)).astype(BF)
    grad_inputs = contract_last(high, places) + contract_last(rest, places)

    out_end = used + down_start
    small_grad = grad_in[:, out_end:]
    deep, quarter = low_up.shape[2], rows // 4
    shared = small_grad + swap(small_grad.astype(BF), "tensor", CORE).astype(F32)
    shared = lax.dynamic_slice_in_dim(shared, member * quarter, quarter, 0)

    return (
        block_out,
        grad_inputs,
        shared[:, NORM_COLUMN],
        grad_in[:, :HEAD_K],
        grad_in[:, HEAD_K : 2 * HEAD_K],
        grad_in[:, 2 * HEAD_K : 2 * HEAD_K + HEAD_V],
        grad_in[:, 2 * HEAD_K + HEAD_V : used],
        shared[:, :rank],
        small_grad[:deep, UP_COLUMN : UP_COLUMN + rank].T[None],
        small_grad[:deep, UP_COLUMN + rank][None],
        shared[: head_gain.shape[0] // 4, HEAD_COLUMN],
        grad_in[:, used:out_end].T,
        shared[:, MLP_COLUMN],
        grad_gu[:, : mlp_gate.shape[1]],
        grad_gu[:, mlp_gate.shape[1] :],
        grad_mlp_down,
    )


def solution(mesh):
    return jax.shard_map(
        local,
        mesh=mesh,
        in_specs=(
            P(("dp", "tensor"), None),
            P("dp"),
            P("dp", "tensor"),
            P("dp", "tensor"),
            P("dp", "tensor"),
            P("dp", "tensor"),
            P("dp", None),
            P("tensor", None, "dp"),
            P("tensor", "dp"),
            P("dp"),
            P("tensor", "dp"),
            P("dp"),
            P("dp", "tensor"),
            P("dp", "tensor"),
            P("tensor", "dp"),
            P(("dp", "tensor"), None),
        ),
        out_specs=(
            P(("dp", "tensor"), None),
            P(("dp", "tensor"), None),
            P(("dp", "tensor")),
            P("dp", "tensor"),
            P("dp", "tensor"),
            P("dp", "tensor"),
            P("dp", "tensor"),
            P(("dp", "tensor"), None),
            P("tensor", None, "dp"),
            P("tensor", "dp"),
            P(("dp", "tensor")),
            P("tensor", "dp"),
            P(("dp", "tensor")),
            P("dp", "tensor"),
            P("dp", "tensor"),
            P("tensor", "dp"),
        ),
        check_vma=False,
    )
```

```python
import jax
import jax.numpy as jnp
from jax import lax
from jax.experimental import pallas as pl
from jax.experimental.pallas import tpu as pltpu
from jax.sharding import PartitionSpec as P

HEAD_K = 128
HEAD_V = 256
CHUNK = 128
TILE = 256
LANES = 128
SAFE_RANGE = 60.0

TOP_PRECISION = lax.Precision.HIGHEST
NORM_EPS = 1e-06
HEAD_EPS = 1e-05
NORMALIZER = 16.0
CORE = 1
PAIR = 2
BF = jnp.bfloat16
F32 = jnp.float32
VMEM_LIMIT = 60 << 20
SHORT = pl.CostEstimate(flops=1 << 20, bytes_accessed=1 << 16, transcendentals=0)


def swap(array, axis, mask):
    size = lax.axis_size(axis)
    return lax.ppermute(array, axis, [(i, i ^ mask) for i in range(size)])


def after(array, *others):
    return lax.optimization_barrier((array, *others))[0]


def after_all(arrays, *others):
    return [after(array, *others) for array in arrays]


def slow_masks():
    mask, result = lax.axis_size("dp") // 2, []
    while mask > 1:
        result.append(mask)
        mask //= 2
    return result


def gather_slow(part, masks):
    for mask in masks:
        part = jnp.concatenate([part, swap(part, "dp", mask)], axis=0)
    return part


def gather_fast(held):
    return swap(held, "dp", 1), swap(held, "tensor", PAIR)


def corner_parts(beside, pair):
    half = pair.shape[0] // 2
    return pair[:half], beside[half:]


def gather_last(held, beside, pair, parts):
    return held, beside, pair, swap(parts[0], "dp", 1), swap(parts[1], "tensor", PAIR)


def send_corner(own, pair):
    return swap(pair[2], "dp", 1), swap(pair[3], "tensor", PAIR)


def send_sides(own, pair, corner, *others):
    low, high = corner
    beside_low = swap(after(own[2], *others), "dp", 1)
    pair_rest = swap(after(pair[1], *others), "tensor", PAIR)
    beside_high = swap((own[3].astype(F32) + after(high, *others).astype(F32)).astype(BF), "dp", 1)
    pair_sum = swap((pair[0].astype(F32) + after(low, *others).astype(F32)).astype(BF), "tensor", PAIR)
    return beside_low, beside_high, pair_sum, pair_rest


def add_sides(own, sides):
    beside_low, beside_high, pair_sum, pair_rest = sides
    return [
        own[0].astype(F32) + beside_low.astype(F32) + pair_sum.astype(F32),
        own[1].astype(F32) + beside_high.astype(F32) + pair_rest.astype(F32),
    ]


def send_slow(kept, given, mask):
    return kept + swap(given.astype(BF), "dp", mask).astype(F32)


def scatter_slow(halves, *others):
    total, given = halves
    if others:
        given = after(given, *others)
    masks = slow_masks()[::-1]
    total = send_slow(total, given, masks[0])
    for mask in masks[1:]:
        rows = total.shape[0] // 2
        total = send_slow(total[:rows], total[rows:], mask)
    return total


def slot_owner(slot):
    count = lax.axis_size("dp")
    bits = count.bit_length() - 1
    delta = sum(((slot >> i) & 1) << (bits - 1 - i) for i in range(bits))
    return delta ^ lax.axis_index("dp")


def place_matrix(width):
    block = width // lax.axis_size("dp")
    feature = lax.broadcasted_iota(jnp.int32, (width, width), 0)
    place = lax.broadcasted_iota(jnp.int32, (width, width), 1)
    return (feature == slot_owner(place // block) * block + place % block).astype(BF)


def small_places(width, length, groups):
    count = lax.axis_size("dp")
    block, deep = width // count, length // count
    place = lax.broadcasted_iota(jnp.int32, (width, length), 0)
    entry = lax.broadcasted_iota(jnp.int32, (width, length), 1)
    inside, room = place % block, block // groups
    held = inside % room < deep // groups
    stands = slot_owner(place // block) * deep + inside // room * (deep // groups) + inside % room
    return (held & (entry == stands)).astype(BF)


def contract_rows(former, latter):
    return lax.dot_general(former, latter, (((0,), (0,)), ((), ())), preferred_element_type=F32)


def contract_last(former, latter):
    return lax.dot_general(former, latter, (((1,), (1,)), ((), ())), preferred_element_type=F32)


def project(former, latter):
    return jnp.dot(former, latter, preferred_element_type=F32)


def exact(former, latter):
    return jnp.dot(former, latter, preferred_element_type=F32, precision=TOP_PRECISION)


def halved(array):
    high = array.astype(BF)
    return high, (array - high.astype(F32)).astype(BF)


def fine_last(former, latter):
    former_high, former_low = halved(former)
    latter_high, latter_low = halved(latter)
    return contract_last(former_high, latter_high) + (
        contract_last(former_high, latter_low) + contract_last(former_low, latter_high)
    )


def positions():
    row = lax.broadcasted_iota(jnp.int32, (CHUNK, CHUNK), 0)
    col = lax.broadcasted_iota(jnp.int32, (CHUNK, CHUNK), 1)
    return row, col


def level_terms(cum, size):
    row, col = positions()
    boundary = row // (2 * size) * (2 * size) + size - 1
    at_boundary = exact((col == boundary).astype(F32), cum)
    fade = jnp.exp(-jnp.abs(cum - at_boundary))
    same = row // (2 * size) == col // (2 * size)
    mask = same & (row % (2 * size) >= size) & (col % (2 * size) < size)
    return fade, mask


def state_kernel(shift, k_own, v_own, k_pair, v_pair, low, up, bias, logits, cums, starts, end, memory):
    n = pl.program_id(0)

    @pl.when(n == 0)
    def _():
        memory[...] = jnp.zeros_like(memory)

    row, col = positions()
    triangle = (row >= col).astype(F32)
    for h, (k_ref, v_ref) in enumerate(((k_own, v_own), (k_pair, v_pair))):
        columns = slice(h * HEAD_K, (h + 1) * HEAD_K)
        logit = exact(low[...], up[h]) + bias[h]
        decay = (jnp.minimum(logit, 0.0) - jnp.log1p(jnp.exp(-jnp.abs(logit)))) / NORMALIZER
        cum = exact(triangle, decay)
        closing = cum[CHUNK - 1 :, :]
        logits[:, columns] = logit
        cums[:, columns] = cum
        starts[0, h] = memory[h]
        faded = (k_ref[...].astype(BF).astype(F32) * jnp.exp(closing - cum)).astype(BF)
        memory[h] = jnp.exp(closing) * memory[h] + contract_rows(v_ref[...].astype(BF), faded)

    @pl.when(n == pl.num_programs(0) - 1)
    def _():
        end[...] = memory[...]


def mix_kernel(
    shift, q_own, k_own, v_own, g_own, q_pair, k_pair, v_pair, g_pair, cums, starts, arrived, gain,
    gated_own, gated_pair, mixed_out, full, scores, passed,
):
    n = pl.program_id(0)

    @pl.when(n == 0)
    def _():
        passed[...] = jnp.zeros_like(passed)

    row, col = positions()
    heads = ((q_own, k_own, v_own, g_own, gated_own), (q_pair, k_pair, v_pair, g_pair, gated_pair))
    lowest = jnp.min(cums[CHUNK - 1 :, :])

    @pl.when(lowest > -SAFE_RANGE)
    def _():
        for h, (q_ref, k_ref, _, _, _) in enumerate(heads):
            cum = cums[:, h * HEAD_K : (h + 1) * HEAD_K]
            middle = cum[CHUNK // 2 : CHUNK // 2 + 1, :]
            q = q_ref[...].astype(BF).astype(F32)
            k = k_ref[...].astype(BF).astype(F32)
            both = fine_last(q * jnp.exp(cum - middle), k * jnp.exp(middle - cum))
            own_score = jnp.sum(q * k, axis=1, keepdims=True)
            scores[h] = jnp.where(row > col, both, jnp.where(row == col, own_score, 0.0))

    @pl.when(lowest <= -SAFE_RANGE)
    def _():
        for h, (q_ref, k_ref, _, _, _) in enumerate(heads):
            cum = cums[:, h * HEAD_K : (h + 1) * HEAD_K]
            q = q_ref[...].astype(BF).astype(F32)
            k = k_ref[...].astype(BF).astype(F32)
            scores[h] = jnp.where(row == col, jnp.sum(q * k, axis=1, keepdims=True), 0.0)

            def level(step, carry):
                fade, mask = level_terms(cum, jnp.int32(1) << step)
                both = fine_last(q * fade, k * fade)
                scores[h] = scores[h] + jnp.where(mask, both, 0.0)
                return carry

            lax.fori_loop(0, CHUNK.bit_length() - 1, level, 0)

    for h, (q_ref, _, v_ref, g_ref, out) in enumerate(heads):
        cum = cums[:, h * HEAD_K : (h + 1) * HEAD_K]
        state = starts[0, h] + jnp.exp(passed[h]) * arrived[h].astype(F32)
        full[0, h] = state.astype(BF)
        passed[h] = passed[h] + cum[CHUNK - 1 :, :]
        q = q_ref[...].astype(BF).astype(F32)
        mixed = project(scores[h].astype(BF), v_ref[...].astype(BF))
        mixed = mixed + fine_last(q * jnp.exp(cum), state)
        mixed = mixed * HEAD_K**-0.5
        mixed_out[:, h * HEAD_V : (h + 1) * HEAD_V] = mixed
        scale = lax.rsqrt(jnp.mean(mixed * mixed, axis=-1, keepdims=True) + HEAD_EPS)
        g = g_ref[...]
        out[...] = (mixed * scale * gain[...] * g * jax.nn.sigmoid(g)).astype(BF)


def gate_back_kernel(
    shift, q_own, g_own, d_own, q_pair, g_pair, d_pair, cums, mixed_in, gain,
    d_mixed, d_gate, ends, first, d_gain, memory,
):
    n = pl.program_id(0)

    @pl.when(n == 0)
    def _():
        memory[...] = jnp.zeros_like(memory)
        d_gain[...] = jnp.zeros_like(d_gain)

    for h, (q_ref, g_ref, d_ref) in enumerate(((q_own, g_own, d_own), (q_pair, g_pair, d_pair))):
        wide = slice(h * HEAD_V, (h + 1) * HEAD_V)
        cum = cums[:, h * HEAD_K : (h + 1) * HEAD_K]
        mixed = mixed_in[:, wide]
        scale = lax.rsqrt(jnp.mean(mixed * mixed, axis=-1, keepdims=True) + HEAD_EPS)
        normal = mixed * scale
        g, grad = g_ref[...], d_ref[...]
        sigmoid = jax.nn.sigmoid(g)
        silu = g * sigmoid
        d_gain[...] += jnp.sum(grad * normal * silu, axis=0, keepdims=True)
        scaled = grad * gain[...]
        d_gate[:, wide] = (scaled * normal * sigmoid * (1.0 + g * (1.0 - sigmoid))).astype(BF)
        scaled = scaled * silu
        back = scale * (scaled - normal * jnp.mean(scaled * normal, axis=-1, keepdims=True))
        back = (back * HEAD_K**-0.5).astype(BF)
        d_mixed[:, wide] = back
        ends[0, h] = memory[h]
        q = q_ref[...].astype(BF).astype(F32)
        faded = (q * jnp.exp(cum)).astype(BF)
        memory[h] = jnp.exp(cum[CHUNK - 1 :, :]) * memory[h] + contract_rows(back, faded)

    @pl.when(n == pl.num_programs(0) - 1)
    def _():
        first[...] = memory[...]


def mix_back_kernel(
    shift, q_own, k_own, v_own, low, q_pair, k_pair, v_pair, cums, logits, full, ends, arrived, up,
    d_mixed, d_gate, back_own, back_pair, d_up, d_bias, d_q, d_k, d_cum, scores, grads, passed,
):
    n = pl.program_id(0)

    @pl.when(n == 0)
    def _():
        passed[...] = jnp.zeros_like(passed)
        d_up[...] = jnp.zeros_like(d_up)
        d_bias[...] = jnp.zeros_like(d_bias)

    row, col = positions()
    heads = ((q_own, k_own, v_own, back_own), (q_pair, k_pair, v_pair, back_pair))
    lowest = jnp.min(cums[CHUNK - 1 :, :])
    for h, (_, _, v_ref, _) in enumerate(heads):
        back = d_mixed[:, h * HEAD_V : (h + 1) * HEAD_V]
        grads[h] = contract_last(back, v_ref[...].astype(BF))

    @pl.when(lowest > -SAFE_RANGE)
    def _():
        for h, (q_ref, k_ref, _, _) in enumerate(heads):
            cum = cums[:, h * HEAD_K : (h + 1) * HEAD_K]
            middle = cum[CHUNK // 2 : CHUNK // 2 + 1, :]
            q = q_ref[...].astype(BF).astype(F32)
            k = k_ref[...].astype(BF).astype(F32)
            rise, fall = jnp.exp(cum - middle), jnp.exp(middle - cum)
            q_faded, k_faded = (q * rise).astype(BF), (k * fall).astype(BF)
            own_score = jnp.sum(q * k, axis=1, keepdims=True)
            both = fine_last(q * rise, k * fall)
            scores[h] = jnp.where(row > col, both, jnp.where(row == col, own_score, 0.0))
            strict = jnp.where(row > col, grads[h], 0.0).astype(BF)
            q_part, k_part = project(strict, k_faded), contract_rows(strict, q_faded)
            d_q[h], d_k[h] = q_part * rise, k_part * fall
            d_cum[h] = q_faded.astype(F32) * q_part - k_faded.astype(F32) * k_part

    @pl.when(lowest <= -SAFE_RANGE)
    def _():
        for h, (q_ref, k_ref, _, _) in enumerate(heads):
            cum = cums[:, h * HEAD_K : (h + 1) * HEAD_K]
            q = q_ref[...].astype(BF).astype(F32)
            k = k_ref[...].astype(BF).astype(F32)
            scores[h] = jnp.where(row == col, jnp.sum(q * k, axis=1, keepdims=True), 0.0)
            d_q[h] = jnp.zeros((CHUNK, HEAD_K), F32)
            d_k[h] = jnp.zeros((CHUNK, HEAD_K), F32)
            d_cum[h] = jnp.zeros((CHUNK, HEAD_K), F32)

            def level(step, carry):
                fade, mask = level_terms(cum, jnp.int32(1) << step)
                q_faded, k_faded = (q * fade).astype(BF), (k * fade).astype(BF)
                scores[h] = scores[h] + jnp.where(mask, fine_last(q * fade, k * fade), 0.0)
                crossing = jnp.where(mask, grads[h], 0.0).astype(BF)
                q_part, k_part = project(crossing, k_faded), contract_rows(crossing, q_faded)
                d_q[h] = d_q[h] + q_part * fade
                d_k[h] = d_k[h] + k_part * fade
                d_cum[h] = d_cum[h] + q_faded.astype(F32) * q_part - k_faded.astype(F32) * k_part
                return carry

            lax.fori_loop(0, CHUNK.bit_length() - 1, level, 0)

    later = (row <= col).astype(F32)
    d_low = jnp.zeros((CHUNK, LANES), F32)
    for h, (q_ref, k_ref, v_ref, out) in enumerate(heads):
        columns = slice(h * HEAD_K, (h + 1) * HEAD_K)
        wide = slice(h * HEAD_V, (h + 1) * HEAD_V)
        cum = cums[:, columns]
        closing = cum[CHUNK - 1 :, :]
        q = q_ref[...].astype(BF).astype(F32)
        k = k_ref[...].astype(BF).astype(F32)
        v, back, state = v_ref[...].astype(BF), d_mixed[:, wide], full[0, h]
        state_grad = ends[0, h] + jnp.exp(passed[h]) * arrived[h].astype(F32)
        passed[h] = passed[h] + closing
        low_grad = state_grad.astype(BF)
        fade = jnp.exp(closing - cum)
        q_state = project(back, state) * jnp.exp(cum)
        k_state = project(v, low_grad) * fade
        diagonal = jnp.sum(jnp.where(row == col, grads[h], 0.0), axis=1, keepdims=True)
        d_v = contract_rows(scores[h].astype(BF), back) + contract_last((k * fade).astype(BF), low_grad)
        d_closing = jnp.sum(k * k_state, axis=0, keepdims=True) + jnp.exp(closing) * jnp.sum(
            state.astype(F32) * state_grad, axis=0, keepdims=True
        )
        d_decay = exact(later, d_cum[h] + q * q_state - k * k_state) + d_closing
        d_logit = d_decay * (jax.nn.sigmoid(-logits[:, columns]) / NORMALIZER)
        out[:, :HEAD_K] = (d_q[h] + q_state + diagonal * k).astype(BF)
        out[:, HEAD_K : 2 * HEAD_K] = (d_k[h] + k_state + diagonal * q).astype(BF)
        out[:, 2 * HEAD_K : 2 * HEAD_K + HEAD_V] = d_v.astype(BF)
        out[:, 2 * HEAD_K + HEAD_V : 2 * HEAD_K + 2 * HEAD_V] = d_gate[:, wide]
        low_logit = d_logit.astype(BF)
        d_low = d_low + contract_last(low_logit, up[h].astype(BF))
        d_up[h] = d_up[h] + contract_rows(low[...].astype(BF), low_logit)
        d_bias[h] = d_bias[h] + jnp.sum(d_logit, axis=0, keepdims=True)
    back_own[:, 2 * HEAD_K + 2 * HEAD_V :] = d_low.astype(BF)


def whole(shape):
    return pl.BlockSpec(shape, lambda n, shift: (0,) * len(shape))


def call(kernel, steps, ins, outs, scratch, arrays, shift, backward=False):
    def at(n):
        return steps - 1 - n if backward else n

    def spec(entry):
        shape, kind, column = entry
        if kind == "r":
            return pl.BlockSpec(shape, lambda n, shift: ((at(n) + shift[0]) % steps, column))
        if kind == "t":
            return pl.BlockSpec(shape, lambda n, shift: (at(n),) + (0,) * (len(shape) - 1))
        return whole(shape)

    shapes = []
    for (shape, kind, _), dtype in outs:
        shapes.append(jax.ShapeDtypeStruct((shape[0] * (steps if kind != "w" else 1),) + shape[1:], dtype))
    return pl.pallas_call(
        kernel,
        grid_spec=pltpu.PrefetchScalarGridSpec(
            num_scalar_prefetch=1,
            grid=(steps,),
            in_specs=[spec(entry) for entry in ins],
            out_specs=[spec(entry) for entry, _ in outs],
            scratch_shapes=scratch,
        ),
        out_shape=shapes,
        compiler_params=pltpu.CompilerParams(vmem_limit_bytes=VMEM_LIMIT),
        cost_estimate=SHORT,
    )(shift, *arrays)


NARROW, WIDE = (CHUNK, HEAD_K), (CHUNK, HEAD_V)
STATES = (1, 2, HEAD_V, HEAD_K)
Q, K, V, G = (NARROW, "r", 0), (NARROW, "r", 1), (WIDE, "r", 1), (WIDE, "r", 2)
LOW = (NARROW, "r", (2 * HEAD_K + 2 * HEAD_V) // LANES)
CUMS = ((CHUNK, 2 * HEAD_K), "t", 0)
HEADS_WIDE = ((CHUNK, 2 * HEAD_V), "t", 0)
STATE = ((2, HEAD_V, HEAD_K), "w", 0)
SQUARES = pltpu.VMEM((2, CHUNK, CHUNK), F32)
NARROWS = pltpu.VMEM((2, CHUNK, HEAD_K), F32)
MEMORY = pltpu.VMEM((2, HEAD_V, HEAD_K), F32)
PASSED = pltpu.VMEM((2, 1, HEAD_K), F32)
UP = ((2, LANES, HEAD_K), "w", 0)
BIAS = ((2, 1, HEAD_K), "w", 0)
GAIN = ((1, HEAD_V), "w", 0)
RISE = ((0, 2), (1, 3))
FALL = ((2, 0), (3, 1))


def mixer(own, pair, up, bias, gain, shift):
    steps = own.shape[0] // CHUNK
    logits, cums, starts, end = call(
        state_kernel,
        steps,
        [K, V, K, V, LOW, UP, BIAS],
        [(CUMS, F32), (CUMS, F32), ((STATES, "t", 0), F32), (STATE, F32)],
        [MEMORY],
        (own, own, pair, pair, own, up, bias),
        shift,
    )
    arrived = lax.ppermute(end[::-1].astype(BF), "tensor", RISE)
    gated_own, gated_pair, mixed, full = call(
        mix_kernel,
        steps,
        [Q, K, V, G, Q, K, V, G, CUMS, (STATES, "t", 0), STATE, GAIN],
        [((WIDE, "r", 0), BF), ((WIDE, "r", 0), BF), (HEADS_WIDE, F32), ((STATES, "t", 0), BF)],
        [SQUARES, PASSED],
        (own, own, own, own, pair, pair, pair, pair, cums, starts, arrived, gain),
        shift,
    )
    return gated_own, gated_pair, (logits, cums, mixed, full)


def mixer_back_first(own, pair, gain, shift, kept, d_own, d_pair):
    _, cums, mixed, _ = kept
    grad = (WIDE, "r", 0)
    return call(
        gate_back_kernel,
        own.shape[0] // CHUNK,
        [Q, G, grad, Q, G, grad, CUMS, HEADS_WIDE, GAIN],
        [(HEADS_WIDE, BF), (((CHUNK, 2 * HEAD_V), "r", 0), BF), ((STATES, "t", 0), F32), (STATE, F32), (GAIN, F32)],
        [MEMORY],
        (own, own, d_own, pair, pair, d_pair, cums, mixed, gain),
        shift,
        backward=True,
    )


def mixer_back_second(own, pair, up, shift, kept, ends, arrived, d_mixed, d_gate):
    logits, cums, _, full = kept
    return call(
        mix_back_kernel,
        own.shape[0] // CHUNK,
        [Q, K, V, LOW, Q, K, V, CUMS, CUMS, (STATES, "t", 0), (STATES, "t", 0), STATE, UP, HEADS_WIDE]
        + [((CHUNK, 2 * HEAD_V), "r", 0)],
        [
            (((CHUNK, own.shape[1]), "r", 0), BF),
            (((CHUNK, pair.shape[1]), "r", 0), BF),
            (UP, F32),
            (BIAS, F32),
        ],
        [NARROWS, NARROWS, NARROWS, SQUARES, SQUARES, PASSED],
        (own, own, own, own, pair, pair, pair, cums, logits, full, ends, arrived, up, d_mixed, d_gate),
        shift,
        backward=True,
    )


def matmul_call(kernel, steps, ins, outs, arrays):
    return pl.pallas_call(
        kernel,
        grid=(steps,),
        in_specs=[pl.BlockSpec(shape, index) for shape, index in ins],
        out_specs=[pl.BlockSpec(shape, index) for (shape, index), _ in outs],
        out_shape=[shape for _, shape in outs],
        compiler_params=pltpu.CompilerParams(vmem_limit_bytes=VMEM_LIMIT),
        cost_estimate=SHORT,
    )(*arrays)


def fixed(array):
    return array.shape, lambda n: (0,) * array.ndim


def by_rows(rows, array, start=0):
    return (rows,) + array.shape[1:], lambda n: (n + start, 0)


def transposed(first, second):
    columns, start = first.shape[1], first.shape[0]
    if columns % LANES:
        return jnp.concatenate([first.T, second.T], axis=1)

    def kernel(first_ref, second_ref, out):
        out[:, :start] = first_ref[...].astype(F32).T.astype(BF)
        out[:, start:] = second_ref[...].astype(F32).T.astype(BF)

    out = struct(columns, start + second.shape[0], BF)
    return matmul_call(kernel, 1, [fixed(first), fixed(second)], [(fixed(out), out)], (first, second))[0]


def struct(rows, columns, kind):
    return jax.ShapeDtypeStruct((rows, columns), kind)


def split_rows(x):
    half, quarter = x.shape[1] // 2, x.shape[1] // 4
    return x[:, :half], x[:, half : half + quarter], x[:, half + quarter :]


def own_product(x, pieces, start, stop):
    half = x.shape[1] // 2
    return project(x[:, :half], pieces[0][:, start:stop]) + project(x[:, half:], pieces[1][:, start:stop])


def pair_product(x, pieces, start, stop):
    first, second, third = split_rows(x)
    return (
        project(first, pieces[2][:, start:stop])
        + project(second, pieces[3][:, start:stop])
        + project(third, pieces[4][:, start:stop])
    )


def project_in(rows, pieces, used):
    tokens = rows.shape[0]
    columns = pieces[0].shape[1]
    tile = min(TILE, tokens)

    def kernel(x_ref, *refs):
        own, pair = refs[5:]
        x = x_ref[...]
        own[...] = own_product(x, refs, 0, columns)
        pair[...] = pair_product(x, refs, 0, used)

    outs = [struct(tokens, columns, F32), struct(tokens, used, F32)]
    return matmul_call(
        kernel,
        tokens // tile,
        [by_rows(tile, rows)] + [fixed(p) for p in pieces],
        [(by_rows(tile, o), o) for o in outs],
        (rows, *pieces),
    )


def project_out(own, pair, pieces, start, parts):
    width = 2 * pieces[0].shape[0]
    quarter = width // 4
    own_stop, pair_stop = start + own.shape[1], start + pair.shape[1]

    def kernel(own_ref, pair_ref, a, b, c, d, e, *outs):
        n = pl.program_id(0)
        for j, (mine, other) in enumerate(((a, c), (a, c), (b, d), (b, e))):

            @pl.when(n == j)
            def _():
                own_weight, pair_weight = mine[:, start:own_stop], other[:, start:pair_stop]
                for out, (first, rows, kind) in zip(outs, parts):
                    lines = slice(first, first + rows)
                    out[...] = (
                        contract_last(own_ref[lines, :], own_weight) + contract_last(pair_ref[lines, :], pair_weight)
                    ).astype(kind)

    def streamed(piece, first):
        last = piece.shape[0] // quarter - 1
        return (quarter, piece.shape[1]), lambda n: (jnp.clip(n - first, 0, last), 0)

    outs = [struct(rows, width, kind) for _, rows, kind in parts]
    return matmul_call(
        kernel,
        4,
        [fixed(own), fixed(pair)] + [streamed(p, first) for p, first in zip(pieces, (0, 2, 0, 2, 3))],
        [(((o.shape[0], quarter), lambda n: (0, n)), o) for o in outs],
        (own, pair, *pieces),
    )


def hidden_products(rows, cot, pieces, down, start):
    tokens, width = rows.shape
    units = pieces[0].shape[1] // 2
    tile = min(TILE, tokens)

    def kernel(x_ref, c_ref, *refs):
        both, downs, outs = refs[:5], refs[5:10], refs[10:]
        x, c = x_ref[...], c_ref[...]
        for h, product in enumerate((own_product, pair_product)):
            hidden, back = outs[2 * h : 2 * h + 2]
            gate_up = product(x, both, 0, 2 * units)
            grad = product(c, downs, start, start + units)
            gate, up = gate_up[:, :units], gate_up[:, units:]
            sigmoid = jax.nn.sigmoid(gate)
            silu = gate * sigmoid
            hidden[...] = (silu * up).astype(BF)
            back[:, :units] = (grad * up * sigmoid * (1.0 + gate * (1.0 - sigmoid))).astype(BF)
            back[:, units:] = (grad * silu).astype(BF)

    outs = [struct(tokens, units, BF), struct(tokens, 2 * units, BF)] * 2
    return matmul_call(
        kernel,
        tokens // tile,
        [by_rows(tile, rows), by_rows(tile, cot)] + [fixed(p) for p in (*pieces, *down)],
        [(by_rows(tile, o), o) for o in outs],
        (rows, cot, *pieces, *down),
    )


def weight_grads(rows, own, pair, pieces=None):
    tokens, width = rows.shape
    quarter = width // 4
    columns = own.shape[1]
    weights = () if pieces is None else tuple(pieces)

    def kernel(x_ref, own_ref, pair_ref, *refs):
        n = pl.program_id(0)
        outs = refs[len(weights) :]
        x = x_ref[...]
        own_grad, pair_grad = contract_rows(x, own_ref[...]), contract_rows(x, pair_ref[...])
        for j in range(4):

            @pl.when(n == j)
            def _():
                outs[j][...] = own_grad.astype(BF)
                outs[4 + j][...] = pair_grad.astype(BF)
                if weights:
                    own_weight, pair_weight = block_of(refs, j, quarter, columns)
                    total = own_grad * own_weight.astype(F32) + pair_grad * pair_weight.astype(F32)
                    total = jnp.sum(total, axis=1, keepdims=True)
                    outs[8][...] = jnp.broadcast_to(total, (quarter, LANES))

    shapes = [struct(quarter, columns, BF)] * 8
    outs = [(fixed(o), o) for o in shapes]
    if weights:
        total = struct(width, LANES, F32)
        outs.append((by_rows(quarter, total), total))
    result = matmul_call(
        kernel,
        4,
        [((tokens, quarter), lambda n: (0, n)), fixed(own), fixed(pair)] + [fixed(p) for p in weights],
        outs,
        (rows, own, pair, *weights),
    )
    return result[:4], result[4:8], result[8:]


def block_of(pieces, j, quarter, columns):
    a, b, c, d, e = pieces[:5]
    own = (a, b)[j // 2][j % 2 * quarter : (j % 2 + 1) * quarter, :columns]
    pair = (c[:quarter, :columns], c[quarter:, :columns], d[:, :columns], e[:, :columns])[j]
    return own, pair


NORM_COLUMN, MLP_COLUMN, HEAD_COLUMN, UP_COLUMN = 16, 17, 18, 32


def gate_weight_grads(rows, gates, cot, gated_own, gated_pair):
    tokens, width = rows.shape
    quarter = width // 4

    def kernel(x_ref, gates, c_ref, gated_o, gated_p, *outs):
        n = pl.program_id(0)
        x, cots = x_ref[...], c_ref[...]
        gate_grad = contract_rows(x, gates[...])
        out_grads = contract_rows(cots, gated_o[...]), contract_rows(cots, gated_p[...])
        for j in range(4):

            @pl.when(n == j)
            def _():
                for h in range(2):
                    outs[4 * h + j][:, :HEAD_V] = gate_grad[:, h * HEAD_V : (h + 1) * HEAD_V].astype(BF)
                    outs[4 * h + j][:, HEAD_V:] = out_grads[h].astype(BF)

    by_columns = ((tokens, quarter), lambda n: (0, n))
    shapes = [struct(quarter, 2 * HEAD_V, BF)] * 8
    result = matmul_call(
        kernel,
        4,
        [by_columns, fixed(gates), by_columns, fixed(gated_own), fixed(gated_pair)],
        [(fixed(o), o) for o in shapes],
        (rows, gates, cot, gated_own, gated_pair),
    )
    return result[:4], result[4:]


def mixer_weight_grads(rows, own, pair, pieces, mlp_total, up, bias, head, places):
    tokens, width = rows.shape
    quarter = width // 4
    used = pair.shape[1]
    kept = used - HEAD_V
    columns = kept + LANES
    rank = UP_COLUMN // 2

    def kernel(
        x_ref, own_ref, pair_ref, a, b, c, d, e, mlp_ref, up_ref, bias_ref,
        head_ref, deep_ref, wide_ref, mine_ref, *outs,
    ):
        n = pl.program_id(0)
        x = x_ref[...]
        own_grad, pair_grad = contract_rows(x, own_ref[...]), contract_rows(x, pair_ref[...])
        column = lax.broadcasted_iota(jnp.int32, (quarter, LANES), 1)
        line = lax.broadcasted_iota(jnp.int32, (LANES, HEAD_K), 0)
        head_total = jnp.sum(wide_ref[...].astype(F32) * head_ref[...], axis=1, keepdims=True)
        heads = []
        for h in range(2):
            entries = jnp.where(line < rank, up_ref[h], jnp.where(line == rank, bias_ref[h], 0.0))
            entries = jnp.concatenate(
                [jnp.zeros((UP_COLUMN, HEAD_K), F32), entries[: LANES - UP_COLUMN]], axis=0
            ).astype(BF)
            heads.append(contract_last(deep_ref[...], entries))
        for j in range(4):

            @pl.when(n == j)
            def _():
                own_weight, pair_weight = block_of((a, b, c, d, e), j, quarter, own_ref.shape[1])
                small = own_weight[:, used:].astype(F32)
                total = (
                    jnp.sum(own_grad[:, :used] * own_weight[:, :used].astype(F32), axis=1, keepdims=True)
                    + jnp.sum(pair_grad * pair_weight[:, :used].astype(F32), axis=1, keepdims=True)
                    + jnp.sum(small * own_grad[:, used:], axis=1, keepdims=True)
                )
                shared = own_grad[:, used:]
                shared = jnp.where(column == NORM_COLUMN, total / small, shared)
                shared = jnp.where(column == MLP_COLUMN, mlp_ref[...] / small, shared)
                shared = jnp.where(column == HEAD_COLUMN, head_total, shared)
                mine = mine_ref[...] > 0.0
                for h, grad in enumerate((own_grad, pair_grad)):
                    target = outs[4 * h + j]
                    target[:, :kept] = grad[:, :kept].astype(BF)
                    here = mine if h == 0 else jnp.logical_not(mine)
                    target[:, kept:] = (jnp.where(here, shared, 0.0) + heads[h]).astype(BF)

    def blocks(array):
        return by_rows(quarter, array)

    shapes = [struct(quarter, columns, BF)] * 8
    deep, wide, mine = places
    result = matmul_call(
        kernel,
        4,
        [((tokens, quarter), lambda n: (0, n)), fixed(own), fixed(pair)]
        + [fixed(p) for p in pieces]
        + [blocks(mlp_total), fixed(up), fixed(bias), fixed(head), blocks(deep), blocks(wide), blocks(mine)],
        [(fixed(o), o) for o in shapes],
        (rows, own, pair, *pieces, mlp_total, up, bias, head, deep, wide, mine),
    )
    return result[:4], result[4:]


def gated_grads(rows, pieces, stop):
    tokens = rows.shape[0]
    tile = min(TILE, tokens)

    def kernel(x_ref, *refs):
        x = x_ref[...]
        refs[5][...] = own_product(x, refs, 0, stop)
        refs[6][...] = pair_product(x, refs, 0, stop)

    outs = [struct(tokens, stop, F32)] * 2
    return matmul_call(
        kernel,
        tokens // tile,
        [by_rows(tile, rows)] + [fixed(p) for p in pieces],
        [(by_rows(tile, o), o) for o in outs],
        (rows, *pieces),
    )


def norm_back(grad_out, normal, scale, gain):
    scaled_grad = grad_out * gain
    return scale * (scaled_grad - normal * jnp.mean(scaled_grad * normal, axis=-1, keepdims=True))


def add_theirs(mine, theirs):
    return mine + swap(theirs, "tensor", CORE).astype(F32)


def both_cores(mine):
    return jnp.concatenate([mine, swap(mine, "tensor", CORE)], axis=0)


def local(
    tokens,
    norm_gain,
    query_weight,
    key_weight,
    value_weight,
    gate_weight,
    low_down,
    low_up,
    rank_bias,
    head_gain,
    out_weight,
    mlp_gain,
    mlp_gate,
    mlp_up,
    mlp_down,
    cotangent,
):
    count = lax.axis_size("dp")
    rows, rank = low_down.shape
    width = rows * count
    member = lax.axis_index("tensor")
    shift = (member % 2 * (tokens.shape[0] // CHUNK)).astype(jnp.int32).reshape(1)
    used = 2 * HEAD_K + 2 * HEAD_V

    def column_at(array, start, total):
        array = array if array.ndim == 2 else array[:, None]
        return jnp.pad(array, ((0, rows - array.shape[0]), (start, total - start - array.shape[1])))

    spaced = jnp.pad(head_gain.reshape(4, -1), ((0, 0), (0, (rows - head_gain.shape[0]) // 4))).reshape(-1)
    total = used + LANES
    mixer_part = column_at(query_weight, 0, total)
    for array, start in (
        (key_weight, HEAD_K),
        (value_weight, 2 * HEAD_K),
        (gate_weight, 2 * HEAD_K + HEAD_V),
        (low_down, used),
        (norm_gain, used + NORM_COLUMN),
        (mlp_gain, used + MLP_COLUMN),
        (spaced, used + HEAD_COLUMN),
        (low_up[0].T, used + UP_COLUMN),
        (rank_bias.T, used + UP_COLUMN + rank),
    ):
        mixer_part = mixer_part + column_at(array, start, total)
    masks = slow_masks()
    mixer_held = gather_slow(mixer_part, masks)
    mixer_fast = gather_fast(mixer_held)
    down_held = gather_slow(after(transposed(out_weight, mlp_down), mixer_held), masks[:-1])
    up_held = gather_slow(after(jnp.concatenate([mlp_gate, mlp_up], axis=1), down_held), masks[:-1])
    parts = corner_parts(*mixer_fast)
    mixer_in = gather_last(mixer_held, *mixer_fast, parts)
    down_held = gather_slow(after(down_held, *parts), masks[-1:])
    up_held = gather_slow(after(up_held, down_held), masks[-1:])
    down_held = after(down_held, *mixer_in[3:])
    down_fast = gather_fast(down_held)
    parts = corner_parts(*down_fast)
    down = gather_last(down_held, *down_fast, parts)
    up_held = after(up_held, *parts)
    up_fast = gather_fast(up_held)
    gate_up = gather_last(up_held, *up_fast, corner_parts(*up_fast))
    down_start = out_weight.shape[0]

    places = place_matrix(width)
    deep_places = small_places(width, HEAD_K, 1)
    wide_places = small_places(width, HEAD_V, 4)
    place = lax.broadcasted_iota(jnp.int32, (width, LANES), 0)
    mine_places = (place % rows // (rows // 2) == member // 2).astype(F32)
    tokens = project(tokens, places).astype(BF)
    tokens = after(tokens, deep_places, wide_places, mine_places)
    cot_mine = project(cotangent, places).astype(BF)
    cot_rows = both_cores(cot_mine)

    small_own = jnp.concatenate([p[:, used:] for p in mixer_in[:2]], axis=0)
    small_pair = jnp.concatenate([p[:, used:] for p in mixer_in[2:]], axis=0)
    gain_one = small_own[:, NORM_COLUMN].astype(F32)
    gain_two = small_own[:, MLP_COLUMN].astype(F32)
    heads = jnp.stack([contract_rows(s, deep_places) for s in (small_own, small_pair)])
    up = jnp.pad(heads[:, UP_COLUMN : UP_COLUMN + rank], ((0, 0), (0, LANES - rank), (0, 0)))
    bias = heads[:, UP_COLUMN + rank : UP_COLUMN + rank + 1]
    gain_head = contract_rows(small_own[:, HEAD_COLUMN : HEAD_COLUMN + 1], wide_places)

    inputs = tokens.astype(F32)
    scale_one = lax.rsqrt(jnp.mean(inputs * inputs, axis=-1, keepdims=True) + NORM_EPS)
    normal_one = inputs * scale_one
    normed_rows = both_cores((normal_one * gain_one).astype(BF))
    proj_own, proj_pair = project_in(normed_rows, mixer_in, used)
    gated_own, gated_pair, kept = mixer(proj_own, proj_pair, up, bias, gain_head, shift)
    half = tokens.shape[0]
    (theirs,) = project_out(gated_own, gated_pair, down, 0, [(half, half, BF)])
    (mine,) = project_out(gated_own, gated_pair, down, 0, [(0, half, F32)])
    middle = inputs + add_theirs(mine, theirs)
    scale_two = lax.rsqrt(jnp.mean(middle * middle, axis=-1, keepdims=True) + NORM_EPS)
    normal_two = middle * scale_two
    mlp_rows = both_cores((normal_two * gain_two).astype(BF))
    both_parts = [(half, half, BF), (0, half, F32)]

    hidden_own, back_gu_own, hidden_pair, back_gu_pair = hidden_products(mlp_rows, cot_rows, gate_up, down, down_start)
    theirs, mine = project_out(back_gu_own, back_gu_pair, gate_up, 0, both_parts)
    grad_second = add_theirs(mine, theirs)
    grad_down_own, grad_down_pair, _ = weight_grads(cot_rows, after(hidden_own, theirs), hidden_pair)
    down_corner = send_corner(grad_down_own, grad_down_pair)
    grad_gu_own, grad_gu_pair, (mlp_total,) = weight_grads(
        mlp_rows, after(back_gu_own, grad_down_own[0]), back_gu_pair, gate_up
    )
    down_sides = send_sides(grad_down_own, grad_down_pair, down_corner)
    gu_corner = send_corner(grad_gu_own, grad_gu_pair)
    grad_middle = cot_mine.astype(F32) + norm_back(grad_second, normal_two, scale_two, gain_two)
    mixer_cot = both_cores(grad_middle.astype(BF))

    d_own, d_pair = gated_grads(after(mixer_cot, *down_sides, *gu_corner), down, down_start)
    down_sum = scatter_slow(add_sides(grad_down_own, down_sides), d_own)
    gu_sides = send_sides(grad_gu_own, grad_gu_pair, gu_corner, d_own)
    d_mixed, d_gate, ends, first, d_gain = mixer_back_first(proj_own, proj_pair, gain_head, shift, kept, d_own, d_pair)
    arrived = lax.ppermute(first[::-1].astype(BF), "tensor", FALL)
    gate_own, gate_pair = gate_weight_grads(normed_rows, d_gate, mixer_cot, gated_own, gated_pair)
    back_own, back_pair, d_up, d_bias = mixer_back_second(
        proj_own, proj_pair, up, shift, kept, ends, after(arrived, gate_own[0], down_sum), d_mixed, d_gate
    )
    gate_corner = send_corner(gate_own, after_all(gate_pair, d_bias))
    gu_halves = add_sides(grad_gu_own, gu_sides)
    gu_halves[1] = gu_halves[1].astype(BF)
    back_own = after(back_own, gu_halves[1])
    gu_sum = scatter_slow(gu_halves)

    own_blocks, pair_blocks = mixer_weight_grads(
        normed_rows, back_own, back_pair, mixer_in, mlp_total, d_up, d_bias, d_gain,
        (deep_places, wide_places, mine_places),
    )
    mixer_corner = send_corner(own_blocks, pair_blocks)
    theirs, mine = project_out(after(back_own, own_blocks[0]), back_pair, mixer_in, 0, both_parts)
    gate_sides = send_sides(gate_own, gate_pair, gate_corner, theirs)
    mixer_sides = send_sides(own_blocks, pair_blocks, mixer_corner, mine)
    gate_sum = scatter_slow(add_sides(gate_own, gate_sides), mine)
    grad_normed = add_theirs(mine, theirs)
    theirs, mine = project_out(after(hidden_own, theirs), hidden_pair, down, down_start, both_parts)
    mixer_sum = scatter_slow(add_sides(own_blocks, mixer_sides), mine)
    outputs = middle + add_theirs(mine, theirs)
    block_out = contract_last(outputs.astype(BF), places).astype(BF)
    grad_inputs = grad_middle + norm_back(grad_normed, normal_one, scale_one, gain_one)
    high = grad_inputs.astype(BF)
    rest = (grad_inputs - high.astype(F32)).astype(BF)
    grad_inputs = contract_last(high, places) + contract_last(rest, places)

    small_grad = mixer_sum[:, 2 * HEAD_K + HEAD_V :]
    deep, quarter = low_up.shape[2], rows // 4
    shared = small_grad + swap(small_grad.astype(BF), "tensor", CORE).astype(F32)
    shared = lax.dynamic_slice_in_dim(shared, member * quarter, quarter, 0)

    return (
        block_out,
        grad_inputs,
        shared[:, NORM_COLUMN],
        mixer_sum[:, :HEAD_K],
        mixer_sum[:, HEAD_K : 2 * HEAD_K],
        mixer_sum[:, 2 * HEAD_K : 2 * HEAD_K + HEAD_V],
        gate_sum[:, :HEAD_V],
        shared[:, :rank],
        small_grad[:deep, UP_COLUMN : UP_COLUMN + rank].T[None],
        small_grad[:deep, UP_COLUMN + rank][None],
        shared[: head_gain.shape[0] // 4, HEAD_COLUMN],
        gate_sum[:, HEAD_V:].T,
        shared[:, MLP_COLUMN],
        gu_sum[:, : mlp_gate.shape[1]],
        gu_sum[:, mlp_gate.shape[1] :],
        down_sum.T,
    )


def solution(mesh):
    return jax.shard_map(
        local,
        mesh=mesh,
        in_specs=(
            P(("dp", "tensor"), None),
            P("dp"),
            P("dp", "tensor"),
            P("dp", "tensor"),
            P("dp", "tensor"),
            P("dp", "tensor"),
            P("dp", None),
            P("tensor", None, "dp"),
            P("tensor", "dp"),
            P("dp"),
            P("tensor", "dp"),
            P("dp"),
            P("dp", "tensor"),
            P("dp", "tensor"),
            P("tensor", "dp"),
            P(("dp", "tensor"), None),
        ),
        out_specs=(
            P(("dp", "tensor"), None),
            P(("dp", "tensor"), None),
            P(("dp", "tensor")),
            P("dp", "tensor"),
            P("dp", "tensor"),
            P("dp", "tensor"),
            P("dp", "tensor"),
            P(("dp", "tensor"), None),
            P("tensor", None, "dp"),
            P("tensor", "dp"),
            P(("dp", "tensor")),
            P("tensor", "dp"),
            P(("dp", "tensor")),
            P("dp", "tensor"),
            P("dp", "tensor"),
            P("tensor", "dp"),
        ),
        check_vma=False,
    )
```

```python
import jax
import jax.numpy as jnp
from jax import lax
from jax.experimental import pallas as pl
from jax.experimental.pallas import tpu as pltpu
from jax.sharding import PartitionSpec as P

HEAD_K = 128
HEAD_V = 256
CHUNK = 128
TILE = 256
LANES = 128
SAFE_RANGE = 60.0

TOP_PRECISION = lax.Precision.HIGHEST
NORM_EPS = 1e-06
HEAD_EPS = 1e-05
NORMALIZER = 16.0
CORE = 1
PAIR = 2
BF = jnp.bfloat16
F32 = jnp.float32
VMEM_LIMIT = 60 << 20
SHORT = pl.CostEstimate(flops=1 << 20, bytes_accessed=1 << 16, transcendentals=0)


def swap(array, axis, mask):
    size = lax.axis_size(axis)
    return lax.ppermute(array, axis, [(i, i ^ mask) for i in range(size)])


def after(array, *others):
    return lax.optimization_barrier((array, *others))[0]


def after_all(arrays, *others):
    return [after(array, *others) for array in arrays]


def slow_masks():
    mask, result = lax.axis_size("dp") // 2, []
    while mask > 1:
        result.append(mask)
        mask //= 2
    return result


def gather_slow(part, masks):
    for mask in masks:
        part = jnp.concatenate([part, swap(part, "dp", mask)], axis=0)
    return part


def gather_fast(held):
    return swap(held, "dp", 1), swap(held, "tensor", PAIR)


def corner_parts(beside, pair):
    half = pair.shape[0] // 2
    return pair[:half], beside[half:]


def gather_last(held, beside, pair, parts):
    return held, beside, pair, swap(parts[0], "dp", 1), swap(parts[1], "tensor", PAIR)


def send_corner(own, pair):
    return swap(pair[2], "dp", 1), swap(pair[3], "tensor", PAIR)


def send_sides(own, pair, corner, *others):
    low, high = corner
    beside_low = swap(after(own[2], *others), "dp", 1)
    pair_rest = swap(after(pair[1], *others), "tensor", PAIR)
    beside_high = swap((own[3].astype(F32) + after(high, *others).astype(F32)).astype(BF), "dp", 1)
    pair_sum = swap((pair[0].astype(F32) + after(low, *others).astype(F32)).astype(BF), "tensor", PAIR)
    return beside_low, beside_high, pair_sum, pair_rest


def add_sides(own, sides):
    beside_low, beside_high, pair_sum, pair_rest = sides
    return [
        own[0].astype(F32) + beside_low.astype(F32) + pair_sum.astype(F32),
        own[1].astype(F32) + beside_high.astype(F32) + pair_rest.astype(F32),
    ]


def send_slow(kept, given, mask):
    return kept + swap(given.astype(BF), "dp", mask).astype(F32)


def scatter_slow(halves, *others):
    total, given = halves
    if others:
        given = after(given, *others)
    return scatter_rest(send_slow(total, given, slow_masks()[-1]))


def scatter_rest(total):
    for mask in slow_masks()[-2::-1]:
        rows = total.shape[0] // 2
        total = send_slow(total[:rows], total[rows:], mask)
    return total


def slot_owner(slot):
    count = lax.axis_size("dp")
    bits = count.bit_length() - 1
    delta = sum(((slot >> i) & 1) << (bits - 1 - i) for i in range(bits))
    return delta ^ lax.axis_index("dp")


def place_matrix(width):
    block = width // lax.axis_size("dp")
    feature = lax.broadcasted_iota(jnp.int32, (width, width), 0)
    place = lax.broadcasted_iota(jnp.int32, (width, width), 1)
    return (feature == slot_owner(place // block) * block + place % block).astype(BF)


def small_places(width, length, groups):
    count = lax.axis_size("dp")
    block, deep = width // count, length // count
    place = lax.broadcasted_iota(jnp.int32, (width, length), 0)
    entry = lax.broadcasted_iota(jnp.int32, (width, length), 1)
    inside, room = place % block, block // groups
    held = inside % room < deep // groups
    stands = slot_owner(place // block) * deep + inside // room * (deep // groups) + inside % room
    return (held & (entry == stands)).astype(BF)


def contract_rows(former, latter):
    return lax.dot_general(former, latter, (((0,), (0,)), ((), ())), preferred_element_type=F32)


def contract_last(former, latter):
    return lax.dot_general(former, latter, (((1,), (1,)), ((), ())), preferred_element_type=F32)


def project(former, latter):
    return jnp.dot(former, latter, preferred_element_type=F32)


def exact(former, latter):
    return jnp.dot(former, latter, preferred_element_type=F32, precision=TOP_PRECISION)


def halved(array):
    high = array.astype(BF)
    return high, (array - high.astype(F32)).astype(BF)


def fine_last(former, latter):
    former_high, former_low = halved(former)
    latter_high, latter_low = halved(latter)
    return contract_last(former_high, latter_high) + (
        contract_last(former_high, latter_low) + contract_last(former_low, latter_high)
    )


def positions():
    row = lax.broadcasted_iota(jnp.int32, (CHUNK, CHUNK), 0)
    col = lax.broadcasted_iota(jnp.int32, (CHUNK, CHUNK), 1)
    return row, col


def level_terms(cum, size):
    row, col = positions()
    boundary = row // (2 * size) * (2 * size) + size - 1
    at_boundary = exact((col == boundary).astype(F32), cum)
    fade = jnp.exp(-jnp.abs(cum - at_boundary))
    same = row // (2 * size) == col // (2 * size)
    mask = same & (row % (2 * size) >= size) & (col % (2 * size) < size)
    return fade, mask


def state_kernel(shift, k_own, v_own, k_pair, v_pair, low, up, bias, logits, cums, starts, end, memory):
    n = pl.program_id(0)

    @pl.when(n == 0)
    def _():
        memory[...] = jnp.zeros_like(memory)

    row, col = positions()
    triangle = (row >= col).astype(F32)
    for h, (k_ref, v_ref) in enumerate(((k_own, v_own), (k_pair, v_pair))):
        columns = slice(h * HEAD_K, (h + 1) * HEAD_K)
        logit = exact(low[...], up[h]) + bias[h]
        decay = (jnp.minimum(logit, 0.0) - jnp.log1p(jnp.exp(-jnp.abs(logit)))) / NORMALIZER
        cum = exact(triangle, decay)
        closing = cum[CHUNK - 1 :, :]
        logits[:, columns] = logit
        cums[:, columns] = cum
        starts[0, h] = memory[h]
        faded = (k_ref[...].astype(BF).astype(F32) * jnp.exp(closing - cum)).astype(BF)
        memory[h] = jnp.exp(closing) * memory[h] + contract_rows(v_ref[...].astype(BF), faded)

    @pl.when(n == pl.num_programs(0) - 1)
    def _():
        end[...] = memory[...]


def mix_kernel(
    shift, q_own, k_own, v_own, g_own, q_pair, k_pair, v_pair, g_pair, cums, starts, arrived, gain,
    gated_own, gated_pair, mixed_out, full, scores, passed,
):
    n = pl.program_id(0)

    @pl.when(n == 0)
    def _():
        passed[...] = jnp.zeros_like(passed)

    row, col = positions()
    heads = ((q_own, k_own, v_own, g_own, gated_own), (q_pair, k_pair, v_pair, g_pair, gated_pair))
    lowest = jnp.min(cums[CHUNK - 1 :, :])

    @pl.when(lowest > -SAFE_RANGE)
    def _():
        for h, (q_ref, k_ref, _, _, _) in enumerate(heads):
            cum = cums[:, h * HEAD_K : (h + 1) * HEAD_K]
            middle = cum[CHUNK // 2 : CHUNK // 2 + 1, :]
            q = q_ref[...].astype(BF).astype(F32)
            k = k_ref[...].astype(BF).astype(F32)
            both = fine_last(q * jnp.exp(cum - middle), k * jnp.exp(middle - cum))
            own_score = jnp.sum(q * k, axis=1, keepdims=True)
            scores[h] = jnp.where(row > col, both, jnp.where(row == col, own_score, 0.0))

    @pl.when(lowest <= -SAFE_RANGE)
    def _():
        for h, (q_ref, k_ref, _, _, _) in enumerate(heads):
            cum = cums[:, h * HEAD_K : (h + 1) * HEAD_K]
            q = q_ref[...].astype(BF).astype(F32)
            k = k_ref[...].astype(BF).astype(F32)
            scores[h] = jnp.where(row == col, jnp.sum(q * k, axis=1, keepdims=True), 0.0)

            def level(step, carry):
                fade, mask = level_terms(cum, jnp.int32(1) << step)
                both = fine_last(q * fade, k * fade)
                scores[h] = scores[h] + jnp.where(mask, both, 0.0)
                return carry

            lax.fori_loop(0, CHUNK.bit_length() - 1, level, 0)

    for h, (q_ref, _, v_ref, g_ref, out) in enumerate(heads):
        cum = cums[:, h * HEAD_K : (h + 1) * HEAD_K]
        state = starts[0, h] + jnp.exp(passed[h]) * arrived[h].astype(F32)
        full[0, h] = state.astype(BF)
        passed[h] = passed[h] + cum[CHUNK - 1 :, :]
        q = q_ref[...].astype(BF).astype(F32)
        mixed = project(scores[h].astype(BF), v_ref[...].astype(BF))
        mixed = mixed + fine_last(q * jnp.exp(cum), state)
        mixed = mixed * HEAD_K**-0.5
        mixed_out[:, h * HEAD_V : (h + 1) * HEAD_V] = mixed
        scale = lax.rsqrt(jnp.mean(mixed * mixed, axis=-1, keepdims=True) + HEAD_EPS)
        g = g_ref[...]
        out[...] = (mixed * scale * gain[...] * g * jax.nn.sigmoid(g)).astype(BF)


def gate_back_kernel(
    shift, q_own, g_own, d_own, q_pair, g_pair, d_pair, cums, mixed_in, gain,
    d_mixed, d_gate, ends, first, d_gain, memory,
):
    n = pl.program_id(0)

    @pl.when(n == 0)
    def _():
        memory[...] = jnp.zeros_like(memory)
        d_gain[...] = jnp.zeros_like(d_gain)

    for h, (q_ref, g_ref, d_ref) in enumerate(((q_own, g_own, d_own), (q_pair, g_pair, d_pair))):
        wide = slice(h * HEAD_V, (h + 1) * HEAD_V)
        cum = cums[:, h * HEAD_K : (h + 1) * HEAD_K]
        mixed = mixed_in[:, wide]
        scale = lax.rsqrt(jnp.mean(mixed * mixed, axis=-1, keepdims=True) + HEAD_EPS)
        normal = mixed * scale
        g, grad = g_ref[...], d_ref[...]
        sigmoid = jax.nn.sigmoid(g)
        silu = g * sigmoid
        d_gain[...] += jnp.sum(grad * normal * silu, axis=0, keepdims=True)
        scaled = grad * gain[...]
        d_gate[:, wide] = (scaled * normal * sigmoid * (1.0 + g * (1.0 - sigmoid))).astype(BF)
        scaled = scaled * silu
        back = scale * (scaled - normal * jnp.mean(scaled * normal, axis=-1, keepdims=True))
        back = (back * HEAD_K**-0.5).astype(BF)
        d_mixed[:, wide] = back
        ends[0, h] = memory[h]
        q = q_ref[...].astype(BF).astype(F32)
        faded = (q * jnp.exp(cum)).astype(BF)
        memory[h] = jnp.exp(cum[CHUNK - 1 :, :]) * memory[h] + contract_rows(back, faded)

    @pl.when(n == pl.num_programs(0) - 1)
    def _():
        first[...] = memory[...]


def mix_back_kernel(
    shift, q_own, k_own, v_own, low, q_pair, k_pair, v_pair, cums, logits, full, ends, arrived, up,
    d_mixed, d_gate, back_own, back_pair, d_up, d_bias, d_q, d_k, d_cum, scores, grads, passed,
):
    n = pl.program_id(0)

    @pl.when(n == 0)
    def _():
        passed[...] = jnp.zeros_like(passed)
        d_up[...] = jnp.zeros_like(d_up)
        d_bias[...] = jnp.zeros_like(d_bias)

    row, col = positions()
    heads = ((q_own, k_own, v_own, back_own), (q_pair, k_pair, v_pair, back_pair))
    lowest = jnp.min(cums[CHUNK - 1 :, :])
    for h, (_, _, v_ref, _) in enumerate(heads):
        back = d_mixed[:, h * HEAD_V : (h + 1) * HEAD_V]
        grads[h] = contract_last(back, v_ref[...].astype(BF))

    @pl.when(lowest > -SAFE_RANGE)
    def _():
        for h, (q_ref, k_ref, _, _) in enumerate(heads):
            cum = cums[:, h * HEAD_K : (h + 1) * HEAD_K]
            middle = cum[CHUNK // 2 : CHUNK // 2 + 1, :]
            q = q_ref[...].astype(BF).astype(F32)
            k = k_ref[...].astype(BF).astype(F32)
            rise, fall = jnp.exp(cum - middle), jnp.exp(middle - cum)
            q_faded, k_faded = (q * rise).astype(BF), (k * fall).astype(BF)
            own_score = jnp.sum(q * k, axis=1, keepdims=True)
            both = fine_last(q * rise, k * fall)
            scores[h] = jnp.where(row > col, both, jnp.where(row == col, own_score, 0.0))
            strict = jnp.where(row > col, grads[h], 0.0).astype(BF)
            q_part, k_part = project(strict, k_faded), contract_rows(strict, q_faded)
            d_q[h], d_k[h] = q_part * rise, k_part * fall
            d_cum[h] = q_faded.astype(F32) * q_part - k_faded.astype(F32) * k_part

    @pl.when(lowest <= -SAFE_RANGE)
    def _():
        for h, (q_ref, k_ref, _, _) in enumerate(heads):
            cum = cums[:, h * HEAD_K : (h + 1) * HEAD_K]
            q = q_ref[...].astype(BF).astype(F32)
            k = k_ref[...].astype(BF).astype(F32)
            scores[h] = jnp.where(row == col, jnp.sum(q * k, axis=1, keepdims=True), 0.0)
            d_q[h] = jnp.zeros((CHUNK, HEAD_K), F32)
            d_k[h] = jnp.zeros((CHUNK, HEAD_K), F32)
            d_cum[h] = jnp.zeros((CHUNK, HEAD_K), F32)

            def level(step, carry):
                fade, mask = level_terms(cum, jnp.int32(1) << step)
                q_faded, k_faded = (q * fade).astype(BF), (k * fade).astype(BF)
                scores[h] = scores[h] + jnp.where(mask, fine_last(q * fade, k * fade), 0.0)
                crossing = jnp.where(mask, grads[h], 0.0).astype(BF)
                q_part, k_part = project(crossing, k_faded), contract_rows(crossing, q_faded)
                d_q[h] = d_q[h] + q_part * fade
                d_k[h] = d_k[h] + k_part * fade
                d_cum[h] = d_cum[h] + q_faded.astype(F32) * q_part - k_faded.astype(F32) * k_part
                return carry

            lax.fori_loop(0, CHUNK.bit_length() - 1, level, 0)

    later = (row <= col).astype(F32)
    d_low = jnp.zeros((CHUNK, LANES), F32)
    for h, (q_ref, k_ref, v_ref, out) in enumerate(heads):
        columns = slice(h * HEAD_K, (h + 1) * HEAD_K)
        wide = slice(h * HEAD_V, (h + 1) * HEAD_V)
        cum = cums[:, columns]
        closing = cum[CHUNK - 1 :, :]
        q = q_ref[...].astype(BF).astype(F32)
        k = k_ref[...].astype(BF).astype(F32)
        v, back, state = v_ref[...].astype(BF), d_mixed[:, wide], full[0, h]
        state_grad = ends[0, h] + jnp.exp(passed[h]) * arrived[h].astype(F32)
        passed[h] = passed[h] + closing
        low_grad = state_grad.astype(BF)
        fade = jnp.exp(closing - cum)
        q_state = project(back, state) * jnp.exp(cum)
        k_state = project(v, low_grad) * fade
        diagonal = jnp.sum(jnp.where(row == col, grads[h], 0.0), axis=1, keepdims=True)
        d_v = contract_rows(scores[h].astype(BF), back) + contract_last((k * fade).astype(BF), low_grad)
        d_closing = jnp.sum(k * k_state, axis=0, keepdims=True) + jnp.exp(closing) * jnp.sum(
            state.astype(F32) * state_grad, axis=0, keepdims=True
        )
        d_decay = exact(later, d_cum[h] + q * q_state - k * k_state) + d_closing
        d_logit = d_decay * (jax.nn.sigmoid(-logits[:, columns]) / NORMALIZER)
        out[:, :HEAD_K] = (d_q[h] + q_state + diagonal * k).astype(BF)
        out[:, HEAD_K : 2 * HEAD_K] = (d_k[h] + k_state + diagonal * q).astype(BF)
        out[:, 2 * HEAD_K : 2 * HEAD_K + HEAD_V] = d_v.astype(BF)
        out[:, 2 * HEAD_K + HEAD_V : 2 * HEAD_K + 2 * HEAD_V] = d_gate[:, wide]
        low_logit = d_logit.astype(BF)
        d_low = d_low + contract_last(low_logit, up[h].astype(BF))
        d_up[h] = d_up[h] + contract_rows(low[...].astype(BF), low_logit)
        d_bias[h] = d_bias[h] + jnp.sum(d_logit, axis=0, keepdims=True)
    back_own[:, 2 * HEAD_K + 2 * HEAD_V :] = d_low.astype(BF)


def whole(shape):
    return pl.BlockSpec(shape, lambda n, shift: (0,) * len(shape))


def call(kernel, steps, ins, outs, scratch, arrays, shift, backward=False):
    def at(n):
        return steps - 1 - n if backward else n

    def spec(entry):
        shape, kind, column = entry
        if kind == "r":
            return pl.BlockSpec(shape, lambda n, shift: ((at(n) + shift[0]) % steps, column))
        if kind == "t":
            return pl.BlockSpec(shape, lambda n, shift: (at(n),) + (0,) * (len(shape) - 1))
        return whole(shape)

    shapes = []
    for (shape, kind, _), dtype in outs:
        shapes.append(jax.ShapeDtypeStruct((shape[0] * (steps if kind != "w" else 1),) + shape[1:], dtype))
    return pl.pallas_call(
        kernel,
        grid_spec=pltpu.PrefetchScalarGridSpec(
            num_scalar_prefetch=1,
            grid=(steps,),
            in_specs=[spec(entry) for entry in ins],
            out_specs=[spec(entry) for entry, _ in outs],
            scratch_shapes=scratch,
        ),
        out_shape=shapes,
        compiler_params=pltpu.CompilerParams(vmem_limit_bytes=VMEM_LIMIT),
        cost_estimate=SHORT,
    )(shift, *arrays)


NARROW, WIDE = (CHUNK, HEAD_K), (CHUNK, HEAD_V)
STATES = (1, 2, HEAD_V, HEAD_K)
Q, K, V, G = (NARROW, "r", 0), (NARROW, "r", 1), (WIDE, "r", 1), (WIDE, "r", 2)
LOW = (NARROW, "r", (2 * HEAD_K + 2 * HEAD_V) // LANES)
CUMS = ((CHUNK, 2 * HEAD_K), "t", 0)
HEADS_WIDE = ((CHUNK, 2 * HEAD_V), "t", 0)
STATE = ((2, HEAD_V, HEAD_K), "w", 0)
SQUARES = pltpu.VMEM((2, CHUNK, CHUNK), F32)
NARROWS = pltpu.VMEM((2, CHUNK, HEAD_K), F32)
MEMORY = pltpu.VMEM((2, HEAD_V, HEAD_K), F32)
PASSED = pltpu.VMEM((2, 1, HEAD_K), F32)
UP = ((2, LANES, HEAD_K), "w", 0)
BIAS = ((2, 1, HEAD_K), "w", 0)
GAIN = ((1, HEAD_V), "w", 0)
RISE = ((0, 2), (1, 3))
FALL = ((2, 0), (3, 1))


def mixer(own, pair, up, bias, gain, shift, ready):
    steps = own.shape[0] // CHUNK
    logits, cums, starts, end = call(
        state_kernel,
        steps,
        [K, V, K, V, LOW, UP, BIAS],
        [(CUMS, F32), (CUMS, F32), ((STATES, "t", 0), F32), (STATE, F32)],
        [MEMORY],
        (own, own, pair, pair, own, up, bias),
        shift,
    )
    arrived = lax.ppermute(end[::-1].astype(BF), "tensor", RISE)
    arrived = after(arrived, ready)
    gated_own, gated_pair, mixed, full = call(
        mix_kernel,
        steps,
        [Q, K, V, G, Q, K, V, G, CUMS, (STATES, "t", 0), STATE, GAIN],
        [((WIDE, "r", 0), BF), ((WIDE, "r", 0), BF), (HEADS_WIDE, F32), ((STATES, "t", 0), BF)],
        [SQUARES, PASSED],
        (own, own, own, own, pair, pair, pair, pair, cums, starts, arrived, gain),
        shift,
    )
    return gated_own, gated_pair, (logits, cums, mixed, full)


def mixer_back_first(own, pair, gain, shift, kept, d_own, d_pair):
    _, cums, mixed, _ = kept
    grad = (WIDE, "r", 0)
    return call(
        gate_back_kernel,
        own.shape[0] // CHUNK,
        [Q, G, grad, Q, G, grad, CUMS, HEADS_WIDE, GAIN],
        [(HEADS_WIDE, BF), (((CHUNK, 2 * HEAD_V), "r", 0), BF), ((STATES, "t", 0), F32), (STATE, F32), (GAIN, F32)],
        [MEMORY],
        (own, own, d_own, pair, pair, d_pair, cums, mixed, gain),
        shift,
        backward=True,
    )


def mixer_back_second(own, pair, up, shift, kept, ends, arrived, d_mixed, d_gate):
    logits, cums, _, full = kept
    return call(
        mix_back_kernel,
        own.shape[0] // CHUNK,
        [Q, K, V, LOW, Q, K, V, CUMS, CUMS, (STATES, "t", 0), (STATES, "t", 0), STATE, UP, HEADS_WIDE]
        + [((CHUNK, 2 * HEAD_V), "r", 0)],
        [
            (((CHUNK, own.shape[1]), "r", 0), BF),
            (((CHUNK, pair.shape[1]), "r", 0), BF),
            (UP, F32),
            (BIAS, F32),
        ],
        [NARROWS, NARROWS, NARROWS, SQUARES, SQUARES, PASSED],
        (own, own, own, own, pair, pair, pair, cums, logits, full, ends, arrived, up, d_mixed, d_gate),
        shift,
        backward=True,
    )


def matmul_call(kernel, steps, ins, outs, arrays):
    return pl.pallas_call(
        kernel,
        grid=(steps,),
        in_specs=[pl.BlockSpec(shape, index) for shape, index in ins],
        out_specs=[pl.BlockSpec(shape, index) for (shape, index), _ in outs],
        out_shape=[shape for _, shape in outs],
        compiler_params=pltpu.CompilerParams(vmem_limit_bytes=VMEM_LIMIT),
        cost_estimate=SHORT,
    )(*arrays)


def fixed(array):
    return array.shape, lambda n: (0,) * array.ndim


def by_rows(rows, array, start=0):
    return (rows,) + array.shape[1:], lambda n: (n + start, 0)


def transposed(first, second):
    columns, start = first.shape[1], first.shape[0]
    if columns % LANES:
        return jnp.concatenate([first.T, second.T], axis=1)

    def kernel(first_ref, second_ref, out):
        out[:, :start] = first_ref[...].astype(F32).T.astype(BF)
        out[:, start:] = second_ref[...].astype(F32).T.astype(BF)

    out = struct(columns, start + second.shape[0], BF)
    return matmul_call(kernel, 1, [fixed(first), fixed(second)], [(fixed(out), out)], (first, second))[0]


def struct(rows, columns, kind):
    return jax.ShapeDtypeStruct((rows, columns), kind)


def split_rows(x):
    half, quarter = x.shape[1] // 2, x.shape[1] // 4
    return x[:, :half], x[:, half : half + quarter], x[:, half + quarter :]


def own_product(x, pieces, start, stop):
    half = x.shape[1] // 2
    return project(x[:, :half], pieces[0][:, start:stop]) + project(x[:, half:], pieces[1][:, start:stop])


def pair_product(x, pieces, start, stop):
    first, second, third = split_rows(x)
    return (
        project(first, pieces[2][:, start:stop])
        + project(second, pieces[3][:, start:stop])
        + project(third, pieces[4][:, start:stop])
    )


def project_in(rows, pieces, used):
    tokens = rows.shape[0]
    columns = pieces[0].shape[1]
    tile = min(TILE, tokens)

    def kernel(x_ref, *refs):
        own, pair = refs[5:]
        x = x_ref[...]
        own[...] = own_product(x, refs, 0, columns)
        pair[...] = pair_product(x, refs, 0, used)

    outs = [struct(tokens, columns, F32), struct(tokens, used, F32)]
    return matmul_call(
        kernel,
        tokens // tile,
        [by_rows(tile, rows)] + [fixed(p) for p in pieces],
        [(by_rows(tile, o), o) for o in outs],
        (rows, *pieces),
    )


def project_out(own, pair, pieces, start, parts):
    width = 2 * pieces[0].shape[0]
    quarter = width // 4
    own_stop, pair_stop = start + own.shape[1], start + pair.shape[1]

    def kernel(own_ref, pair_ref, a, b, c, d, e, *outs):
        n = pl.program_id(0)
        for j, (mine, other) in enumerate(((a, c), (a, c), (b, d), (b, e))):

            @pl.when(n == j)
            def _():
                own_weight, pair_weight = mine[:, start:own_stop], other[:, start:pair_stop]
                for out, (first, rows, kind) in zip(outs, parts):
                    lines = slice(first, first + rows)
                    out[...] = (
                        contract_last(own_ref[lines, :], own_weight) + contract_last(pair_ref[lines, :], pair_weight)
                    ).astype(kind)

    def streamed(piece, first):
        last = piece.shape[0] // quarter - 1
        return (quarter, piece.shape[1]), lambda n: (jnp.clip(n - first, 0, last), 0)

    outs = [struct(rows, width, kind) for _, rows, kind in parts]
    return matmul_call(
        kernel,
        4,
        [fixed(own), fixed(pair)] + [streamed(p, first) for p, first in zip(pieces, (0, 2, 0, 2, 3))],
        [(((o.shape[0], quarter), lambda n: (0, n)), o) for o in outs],
        (own, pair, *pieces),
    )


def hidden_products(rows, cot, pieces, down, start):
    tokens, width = rows.shape
    units = pieces[0].shape[1] // 2
    tile = min(TILE, tokens)

    def kernel(x_ref, c_ref, *refs):
        both, downs, outs = refs[:5], refs[5:10], refs[10:]
        x, c = x_ref[...], c_ref[...]
        for h, product in enumerate((own_product, pair_product)):
            hidden, back = outs[2 * h : 2 * h + 2]
            gate_up = product(x, both, 0, 2 * units)
            grad = product(c, downs, start, start + units)
            gate, up = gate_up[:, :units], gate_up[:, units:]
            sigmoid = jax.nn.sigmoid(gate)
            silu = gate * sigmoid
            hidden[...] = (silu * up).astype(BF)
            back[:, :units] = (grad * up * sigmoid * (1.0 + gate * (1.0 - sigmoid))).astype(BF)
            back[:, units:] = (grad * silu).astype(BF)

    outs = [struct(tokens, units, BF), struct(tokens, 2 * units, BF)] * 2
    return matmul_call(
        kernel,
        tokens // tile,
        [by_rows(tile, rows), by_rows(tile, cot)] + [fixed(p) for p in (*pieces, *down)],
        [(by_rows(tile, o), o) for o in outs],
        (rows, cot, *pieces, *down),
    )


def weight_grads(rows, own, pair, pieces=None):
    tokens, width = rows.shape
    quarter = width // 4
    columns = own.shape[1]
    weights = () if pieces is None else tuple(pieces)

    def kernel(x_ref, own_ref, pair_ref, *refs):
        n = pl.program_id(0)
        outs = refs[len(weights) :]
        x = x_ref[...]
        own_grad, pair_grad = contract_rows(x, own_ref[...]), contract_rows(x, pair_ref[...])
        for j in range(4):

            @pl.when(n == j)
            def _():
                outs[j][...] = own_grad.astype(BF)
                outs[4 + j][...] = pair_grad.astype(BF)
                if weights:
                    own_weight, pair_weight = block_of(refs, j, quarter, columns)
                    total = own_grad * own_weight.astype(F32) + pair_grad * pair_weight.astype(F32)
                    total = jnp.sum(total, axis=1, keepdims=True)
                    outs[8][...] = jnp.broadcast_to(total, (quarter, LANES))

    shapes = [struct(quarter, columns, BF)] * 8
    outs = [(fixed(o), o) for o in shapes]
    if weights:
        total = struct(width, LANES, F32)
        outs.append((by_rows(quarter, total), total))
    result = matmul_call(
        kernel,
        4,
        [((tokens, quarter), lambda n: (0, n)), fixed(own), fixed(pair)] + [fixed(p) for p in weights],
        outs,
        (rows, own, pair, *weights),
    )
    return result[:4], result[4:8], result[8:]


def block_of(pieces, j, quarter, columns):
    a, b, c, d, e = pieces[:5]
    own = (a, b)[j // 2][j % 2 * quarter : (j % 2 + 1) * quarter, :columns]
    pair = (c[:quarter, :columns], c[quarter:, :columns], d[:, :columns], e[:, :columns])[j]
    return own, pair


NORM_COLUMN, MLP_COLUMN, HEAD_COLUMN, UP_COLUMN = 16, 17, 18, 32


def gate_weight_grads(rows, gates, cot, gated_own, gated_pair):
    tokens, width = rows.shape
    quarter = width // 4

    def kernel(x_ref, gates, c_ref, gated_o, gated_p, *outs):
        n = pl.program_id(0)
        x, cots = x_ref[...], c_ref[...]
        gate_grad = contract_rows(x, gates[...])
        out_grads = contract_rows(cots, gated_o[...]), contract_rows(cots, gated_p[...])
        for j in range(4):

            @pl.when(n == j)
            def _():
                for h in range(2):
                    outs[4 * h + j][:, :HEAD_V] = gate_grad[:, h * HEAD_V : (h + 1) * HEAD_V].astype(BF)
                    outs[4 * h + j][:, HEAD_V:] = out_grads[h].astype(BF)

    by_columns = ((tokens, quarter), lambda n: (0, n))
    shapes = [struct(quarter, 2 * HEAD_V, BF)] * 8
    result = matmul_call(
        kernel,
        4,
        [by_columns, fixed(gates), by_columns, fixed(gated_own), fixed(gated_pair)],
        [(fixed(o), o) for o in shapes],
        (rows, gates, cot, gated_own, gated_pair),
    )
    return result[:4], result[4:]


def mixer_weight_grads(rows, own, pair, pieces, mlp_total, up, bias, head, places):
    tokens, width = rows.shape
    quarter = width // 4
    used = pair.shape[1]
    kept = used - HEAD_V
    columns = kept + LANES
    rank = UP_COLUMN // 2

    def kernel(
        x_ref, own_ref, pair_ref, a, b, c, d, e, mlp_ref, up_ref, bias_ref,
        head_ref, deep_ref, wide_ref, mine_ref, *outs,
    ):
        n = pl.program_id(0)
        x = x_ref[...]
        own_grad, pair_grad = contract_rows(x, own_ref[...]), contract_rows(x, pair_ref[...])
        column = lax.broadcasted_iota(jnp.int32, (quarter, LANES), 1)
        line = lax.broadcasted_iota(jnp.int32, (LANES, HEAD_K), 0)
        head_total = jnp.sum(wide_ref[...].astype(F32) * head_ref[...], axis=1, keepdims=True)
        heads = []
        for h in range(2):
            entries = jnp.where(line < rank, up_ref[h], jnp.where(line == rank, bias_ref[h], 0.0))
            entries = jnp.concatenate(
                [jnp.zeros((UP_COLUMN, HEAD_K), F32), entries[: LANES - UP_COLUMN]], axis=0
            ).astype(BF)
            heads.append(contract_last(deep_ref[...], entries))
        for j in range(4):

            @pl.when(n == j)
            def _():
                own_weight, pair_weight = block_of((a, b, c, d, e), j, quarter, own_ref.shape[1])
                small = own_weight[:, used:].astype(F32)
                total = (
                    jnp.sum(own_grad[:, :used] * own_weight[:, :used].astype(F32), axis=1, keepdims=True)
                    + jnp.sum(pair_grad * pair_weight[:, :used].astype(F32), axis=1, keepdims=True)
                    + jnp.sum(small * own_grad[:, used:], axis=1, keepdims=True)
                )
                shared = own_grad[:, used:]
                shared = jnp.where(column == NORM_COLUMN, total / small, shared)
                shared = jnp.where(column == MLP_COLUMN, mlp_ref[...] / small, shared)
                shared = jnp.where(column == HEAD_COLUMN, head_total, shared)
                mine = mine_ref[...] > 0.0
                for h, grad in enumerate((own_grad, pair_grad)):
                    target = outs[4 * h + j]
                    target[:, :kept] = grad[:, :kept].astype(BF)
                    here = mine if h == 0 else jnp.logical_not(mine)
                    target[:, kept:] = (jnp.where(here, shared, 0.0) + heads[h]).astype(BF)

    def blocks(array):
        return by_rows(quarter, array)

    shapes = [struct(quarter, columns, BF)] * 8
    deep, wide, mine = places
    result = matmul_call(
        kernel,
        4,
        [((tokens, quarter), lambda n: (0, n)), fixed(own), fixed(pair)]
        + [fixed(p) for p in pieces]
        + [blocks(mlp_total), fixed(up), fixed(bias), fixed(head), blocks(deep), blocks(wide), blocks(mine)],
        [(fixed(o), o) for o in shapes],
        (rows, own, pair, *pieces, mlp_total, up, bias, head, deep, wide, mine),
    )
    return result[:4], result[4:]


def gated_grads(rows, pieces, stop):
    tokens = rows.shape[0]
    tile = min(TILE, tokens)

    def kernel(x_ref, *refs):
        x = x_ref[...]
        refs[5][...] = own_product(x, refs, 0, stop)
        refs[6][...] = pair_product(x, refs, 0, stop)

    outs = [struct(tokens, stop, F32)] * 2
    return matmul_call(
        kernel,
        tokens // tile,
        [by_rows(tile, rows)] + [fixed(p) for p in pieces],
        [(by_rows(tile, o), o) for o in outs],
        (rows, *pieces),
    )


def norm_back(grad_out, normal, scale, gain):
    scaled_grad = grad_out * gain
    return scale * (scaled_grad - normal * jnp.mean(scaled_grad * normal, axis=-1, keepdims=True))


def add_theirs(mine, theirs):
    return mine + swap(theirs, "tensor", CORE).astype(F32)


def both_cores(mine):
    return jnp.concatenate([mine, swap(mine, "tensor", CORE)], axis=0)


def local(
    tokens,
    norm_gain,
    query_weight,
    key_weight,
    value_weight,
    gate_weight,
    low_down,
    low_up,
    rank_bias,
    head_gain,
    out_weight,
    mlp_gain,
    mlp_gate,
    mlp_up,
    mlp_down,
    cotangent,
):
    count = lax.axis_size("dp")
    rows, rank = low_down.shape
    width = rows * count
    member = lax.axis_index("tensor")
    shift = (member % 2 * (tokens.shape[0] // CHUNK)).astype(jnp.int32).reshape(1)
    used = 2 * HEAD_K + 2 * HEAD_V

    def column_at(array, start, total):
        array = array if array.ndim == 2 else array[:, None]
        return jnp.pad(array, ((0, rows - array.shape[0]), (start, total - start - array.shape[1])))

    spaced = jnp.pad(head_gain.reshape(4, -1), ((0, 0), (0, (rows - head_gain.shape[0]) // 4))).reshape(-1)
    total = used + LANES
    mixer_part = column_at(query_weight, 0, total)
    for array, start in (
        (key_weight, HEAD_K),
        (value_weight, 2 * HEAD_K),
        (gate_weight, 2 * HEAD_K + HEAD_V),
        (low_down, used),
        (norm_gain, used + NORM_COLUMN),
        (mlp_gain, used + MLP_COLUMN),
        (spaced, used + HEAD_COLUMN),
        (low_up[0].T, used + UP_COLUMN),
        (rank_bias.T, used + UP_COLUMN + rank),
    ):
        mixer_part = mixer_part + column_at(array, start, total)
    masks = slow_masks()
    mixer_held = gather_slow(mixer_part, masks)
    mixer_fast = gather_fast(mixer_held)
    down_held = gather_slow(after(transposed(out_weight, mlp_down), mixer_held), masks[:-1])
    up_held = gather_slow(after(jnp.concatenate([mlp_gate, mlp_up], axis=1), down_held), masks[:-1])
    parts = corner_parts(*mixer_fast)
    mixer_in = gather_last(mixer_held, *mixer_fast, parts)
    down_held = gather_slow(after(down_held, *parts), masks[-1:])
    up_held = gather_slow(after(up_held, down_held), masks[-1:])
    down_held = after(down_held, *mixer_in[3:])
    down_fast = gather_fast(down_held)
    down_start = out_weight.shape[0]

    places = place_matrix(width)
    deep_places = small_places(width, HEAD_K, 1)
    wide_places = small_places(width, HEAD_V, 4)
    place = lax.broadcasted_iota(jnp.int32, (width, LANES), 0)
    mine_places = (place % rows // (rows // 2) == member // 2).astype(F32)
    tokens = project(tokens, places).astype(BF)
    tokens = after(tokens, deep_places, wide_places, mine_places)
    cot_mine = project(cotangent, places).astype(BF)
    cot_rows = both_cores(cot_mine)

    small_own = jnp.concatenate([p[:, used:] for p in mixer_in[:2]], axis=0)
    small_pair = jnp.concatenate([p[:, used:] for p in mixer_in[2:]], axis=0)
    gain_one = small_own[:, NORM_COLUMN].astype(F32)
    gain_two = small_own[:, MLP_COLUMN].astype(F32)
    heads = jnp.stack([contract_rows(s, deep_places) for s in (small_own, small_pair)])
    up = jnp.pad(heads[:, UP_COLUMN : UP_COLUMN + rank], ((0, 0), (0, LANES - rank), (0, 0)))
    bias = heads[:, UP_COLUMN + rank : UP_COLUMN + rank + 1]
    gain_head = contract_rows(small_own[:, HEAD_COLUMN : HEAD_COLUMN + 1], wide_places)

    inputs = tokens.astype(F32)
    scale_one = lax.rsqrt(jnp.mean(inputs * inputs, axis=-1, keepdims=True) + NORM_EPS)
    normal_one = inputs * scale_one
    normed_rows = both_cores((normal_one * gain_one).astype(BF))
    proj_own, proj_pair = project_in(normed_rows, mixer_in, used)
    down_fast = after_all(down_fast, proj_own)
    parts = corner_parts(*down_fast)
    down = gather_last(down_held, *down_fast, parts)
    up_held = after(up_held, *parts)
    up_fast = gather_fast(up_held)
    up_parts = corner_parts(*up_fast)
    gate_up = gather_last(up_held, *up_fast, up_parts)
    gated_own, gated_pair, kept = mixer(proj_own, proj_pair, up, bias, gain_head, shift, up_held)
    half = tokens.shape[0]
    gated_own = after(gated_own, *up_fast)
    (theirs,) = project_out(gated_own, gated_pair, down, 0, [(half, half, BF)])
    (mine,) = project_out(after(gated_own, *up_parts), gated_pair, down, 0, [(0, half, F32)])
    middle = inputs + add_theirs(mine, theirs)
    scale_two = lax.rsqrt(jnp.mean(middle * middle, axis=-1, keepdims=True) + NORM_EPS)
    normal_two = middle * scale_two
    mlp_rows = both_cores((normal_two * gain_two).astype(BF))
    both_parts = [(half, half, BF), (0, half, F32)]

    hidden_own, back_gu_own, hidden_pair, back_gu_pair = hidden_products(mlp_rows, cot_rows, gate_up, down, down_start)
    theirs, mine = project_out(back_gu_own, back_gu_pair, gate_up, 0, both_parts)
    grad_second = add_theirs(mine, theirs)
    grad_down_own, grad_down_pair, _ = weight_grads(cot_rows, after(hidden_own, theirs), hidden_pair)
    down_corner = send_corner(grad_down_own, grad_down_pair)
    grad_gu_own, grad_gu_pair, (mlp_total,) = weight_grads(
        mlp_rows, after(back_gu_own, grad_down_own[0]), back_gu_pair, gate_up
    )
    down_sides = send_sides(grad_down_own, grad_down_pair, down_corner)
    gu_corner = send_corner(grad_gu_own, grad_gu_pair)
    grad_middle = cot_mine.astype(F32) + norm_back(grad_second, normal_two, scale_two, gain_two)
    mixer_cot = both_cores(grad_middle.astype(BF))

    d_own, d_pair = gated_grads(mixer_cot, down, down_start)
    down_sum = scatter_slow(add_sides(grad_down_own, down_sides), d_own)
    gu_sides = send_sides(grad_gu_own, grad_gu_pair, gu_corner, d_own)
    d_mixed, d_gate, ends, first, d_gain = mixer_back_first(proj_own, proj_pair, gain_head, shift, kept, d_own, d_pair)
    arrived = lax.ppermute(first[::-1].astype(BF), "tensor", FALL)
    gates = after(d_gate, *down_sides, *gu_corner)
    gate_own, gate_pair = gate_weight_grads(normed_rows, gates, mixer_cot, gated_own, gated_pair)
    back_own, back_pair, d_up, d_bias = mixer_back_second(
        proj_own, proj_pair, up, shift, kept, ends, after(arrived, gate_own[0]), d_mixed, d_gate
    )
    gate_corner = send_corner(gate_own, after_all(gate_pair, d_bias))
    gu_halves = add_sides(grad_gu_own, gu_sides)
    gu_halves[1] = gu_halves[1].astype(BF)
    back_own = after(back_own, gu_halves[1])
    gu_middle = send_slow(*gu_halves, masks[-1])
    gu_sum = scatter_rest(gu_middle)

    own_blocks, pair_blocks = mixer_weight_grads(
        normed_rows, back_own, back_pair, mixer_in, mlp_total, d_up, d_bias, d_gain,
        (deep_places, wide_places, mine_places),
    )
    mixer_corner = send_corner(own_blocks, pair_blocks)
    theirs, mine = project_out(after(back_own, own_blocks[0]), back_pair, mixer_in, 0, both_parts)
    mixer_sides = send_sides(own_blocks, pair_blocks, mixer_corner, mine)
    grad_normed = add_theirs(mine, theirs)
    theirs, mine = project_out(after(hidden_own, theirs, *mixer_corner, gu_middle), hidden_pair, down, down_start, both_parts)
    mixer_halves = add_sides(own_blocks, mixer_sides)
    mixer_halves[1] = mixer_halves[1].astype(BF)
    mixer_sum = scatter_slow(mixer_halves)
    gate_sides = send_sides(gate_own, gate_pair, gate_corner, mine, mixer_halves[1])
    gate_sum = scatter_slow(add_sides(gate_own, gate_sides))
    outputs = middle + add_theirs(mine, theirs)
    block_out = contract_last(outputs.astype(BF), places).astype(BF)
    grad_inputs = grad_middle + norm_back(grad_normed, normal_one, scale_one, gain_one)
    high = grad_inputs.astype(BF)
    rest = (grad_inputs - high.astype(F32)).astype(BF)
    grad_inputs = contract_last(high, places) + contract_last(rest, places)

    small_grad = mixer_sum[:, 2 * HEAD_K + HEAD_V :]
    deep, quarter = low_up.shape[2], rows // 4
    shared = small_grad + swap(small_grad.astype(BF), "tensor", CORE).astype(F32)
    shared = lax.dynamic_slice_in_dim(shared, member * quarter, quarter, 0)

    return (
        block_out,
        grad_inputs,
        shared[:, NORM_COLUMN],
        mixer_sum[:, :HEAD_K],
        mixer_sum[:, HEAD_K : 2 * HEAD_K],
        mixer_sum[:, 2 * HEAD_K : 2 * HEAD_K + HEAD_V],
        gate_sum[:, :HEAD_V],
        shared[:, :rank],
        small_grad[:deep, UP_COLUMN : UP_COLUMN + rank].T[None],
        small_grad[:deep, UP_COLUMN + rank][None],
        shared[: head_gain.shape[0] // 4, HEAD_COLUMN],
        gate_sum[:, HEAD_V:].T,
        shared[:, MLP_COLUMN],
        gu_sum[:, : mlp_gate.shape[1]],
        gu_sum[:, mlp_gate.shape[1] :],
        down_sum.T,
    )


def solution(mesh):
    return jax.shard_map(
        local,
        mesh=mesh,
        in_specs=(
            P(("dp", "tensor"), None),
            P("dp"),
            P("dp", "tensor"),
            P("dp", "tensor"),
            P("dp", "tensor"),
            P("dp", "tensor"),
            P("dp", None),
            P("tensor", None, "dp"),
            P("tensor", "dp"),
            P("dp"),
            P("tensor", "dp"),
            P("dp"),
            P("dp", "tensor"),
            P("dp", "tensor"),
            P("tensor", "dp"),
            P(("dp", "tensor"), None),
        ),
        out_specs=(
            P(("dp", "tensor"), None),
            P(("dp", "tensor"), None),
            P(("dp", "tensor")),
            P("dp", "tensor"),
            P("dp", "tensor"),
            P("dp", "tensor"),
            P("dp", "tensor"),
            P(("dp", "tensor"), None),
            P("tensor", None, "dp"),
            P("tensor", "dp"),
            P(("dp", "tensor")),
            P("tensor", "dp"),
            P(("dp", "tensor")),
            P("dp", "tensor"),
            P("dp", "tensor"),
            P("tensor", "dp"),
        ),
        check_vma=False,
    )
```
